128 devices in a mesh: floor: 16 (over z, x), slab: 8 (over y, core).
Axes of the slice: x: 4, y: 4, z: 4, core: 2. Of those that a mesh axis runs over, the one named last changes fastest.
Arguments:
- latent: bfloat16 [8, 65536, 128], P('slab', 'floor'), may hold values from -6 to 6
- edge_geom: float32 [8, 3, 1048576], P('slab', None, 'floor'), may hold values from -3 to 3
- edge_recv: int32 [8, 1048576], P('slab', 'floor'), may hold values from 0 to 4095, as said below
- edge_send: int32 [8, 1048576], P('slab', 'floor'), may hold values from 0 to 9215, as said below
- ghost_rows: int32 [8, 160, 512], P('slab', 'floor'), may hold values from 0 to 4095
- dest: int32 [8, 65536], P('slab', 'floor'), may hold values from 0 to 15, as said below
- enc_w1: float32 [4, 128], replicated, may hold values from -3 to 3
- enc_b1: float32 [128], replicated, may hold values from -3 to 3
- enc_w2: bfloat16 [128, 128], replicated, may hold values from -0.5 to 0.5
- pe_w1: bfloat16 [3, 128, 128], replicated, may hold values from -0.3125 to 0.3125
- pe_w2: bfloat16 [128, 128], replicated, may hold values from -0.5 to 0.5
- edge_gain: float32 [128], replicated, may hold values from 0.5 to 1.5
- pn_w1: bfloat16 [2, 128, 128], replicated, may hold values from -0.375 to 0.375
- pn_w2: bfloat16 [128, 128], replicated, may hold values from -0.5 to 0.5
- node_gain: float32 [128], replicated, may hold values from 0.5 to 1.5
Outputs:
- staying: bfloat16 [8, 65536, 128], P('slab', 'floor')
- arrivals: bfloat16 [8, 128, 128, 128], P('slab', 'floor')
The draws below stay inside these ranges and needn't reach their ends.
Inputs may be any that keep to these rules, and one draw needn't show every extreme that they name: A particle's dest is its own brick or one of the bricks one step away in the floor grid (rows and columns each differ by at most 1). At most 128 rows of one brick in one slab have dest equal to any one other brick. `edge_send`: A value v < 4096 names row v of the own brick; v = 4096 + k * 512 + j names slot j of ghost block k of ext. Blocks whose source brick or slab lies outside the grid are never named. `edge_recv`: A brick's edges come in tiles of 2048 entries: every entry of tile t names a row from t * 128 to (t + 1) * 128 - 1 of the own brick.
All inputs are finite; a program needn't handle non-finite values.
Results may differ from the reference program's by a relative error of at most 0.0054.
Values may be sent and summed in bfloat16 or wider, within the bound.
A program may use at most 128 MiB of HBM per device.

```python
from functools import partial
import jax
import jax.numpy as jnp
from jax import lax

D = 128
BCOLS = 4
NEIGH = 16
PART_DEV = 4096
RTILE = 128
GCAP = 512
MCAP = 128
EDGES_DEV = 65536
FLOORS = 16
SLABS = 8
ROWS = 65536
EDGES = 1048576


STEP_ROW = (-1, -1, -1, 0, 0, 1, 1, 1)


STEP_COL = (-1, 0, 1, -1, 1, -1, 0, 1)


def brick_moves():
    bricks = jnp.arange(FLOORS, dtype=jnp.int32)
    step_row = jnp.array(STEP_ROW, dtype=jnp.int32)
    step_col = jnp.array(STEP_COL, dtype=jnp.int32)
    return (bricks // BCOLS, bricks % BCOLS, step_row, step_col)


def shuffle_one(one_key):
    return jax.random.permutation(one_key, PART_DEV)


def draw_edge_recv(key, part):
    key = jax.random.fold_in(key, 31)
    places = jnp.arange(EDGES_DEV, dtype=jnp.int32)
    tile_base = places // (RTILE * NEIGH) * RTILE
    within = jax.random.randint(key, (SLABS, FLOORS, EDGES_DEV), 0, RTILE)
    value = tile_base[None, None, :] + within
    value = value.at[:, :, 0].set(0)
    value = value.at[:, :, EDGES_DEV - 1].set(PART_DEV - 1)
    return value.reshape(SLABS, FLOORS * EDGES_DEV).astype(jnp.int32)


def draw_dest(key, part):
    key = jax.random.fold_in(key, 11)
    key_target, key_count, key_order = jax.random.split(key, 3)
    brick_row, brick_col, step_row, step_col = brick_moves()
    grid_rows = FLOORS // BCOLS
    ahead_row = brick_row[:, None] + step_row[None, :]
    ahead_col = brick_col[:, None] + step_col[None, :]
    present = (ahead_row >= 0) & (ahead_row < grid_rows) & (ahead_col >= 0) & (ahead_col < BCOLS)
    ahead = ahead_row * BCOLS + ahead_col
    target = jax.random.randint(key_target, (), 0, FLOORS)
    counts = jax.random.randint(key_count, (SLABS, FLOORS, 8), MCAP // 4, MCAP + 1)
    counts = jnp.where((ahead == target)[None], MCAP, counts)
    counts = jnp.where(present[None], counts, 0)
    bounds = jnp.cumsum(counts, axis=-1)
    places = jnp.arange(PART_DEV, dtype=jnp.int32)
    which = jnp.sum((places[None, None, :, None] >= bounds[:, :, None, :]).astype(jnp.int32), axis=-1)
    landing = jnp.concatenate([ahead, jnp.arange(FLOORS, dtype=jnp.int32)[:, None]], axis=1)
    landing = jnp.broadcast_to(landing[None, :, None, :], (SLABS, FLOORS, PART_DEV, 9))
    chosen = jnp.take_along_axis(landing, which[..., None], axis=-1)[..., 0]
    order_keys = jax.random.split(key_order, SLABS * FLOORS)
    shuffle = jax.vmap(shuffle_one)(order_keys).reshape(SLABS, FLOORS, PART_DEV)
    chosen = jnp.take_along_axis(chosen, shuffle, axis=-1)
    return chosen.reshape(SLABS, FLOORS * PART_DEV).astype(jnp.int32)


def draw_edge_send(key, part):
    key = jax.random.fold_in(key, 23)
    key_target, key_slab, key_live, key_pick = jax.random.split(key, 4)
    brick_row, brick_col, step_row, step_col = brick_moves()
    grid_rows = FLOORS // BCOLS
    behind_row = brick_row[:, None] - step_row[None, :]
    behind_col = brick_col[:, None] - step_col[None, :]
    floor_present = (behind_row >= 0) & (behind_row < grid_rows) & (behind_col >= 0) & (behind_col < BCOLS)
    slab_ids = jnp.arange(SLABS, dtype=jnp.int32)
    slab_present = jnp.stack([slab_ids + 1 < SLABS, slab_ids >= 1], axis=1)
    present = jnp.concatenate([jnp.broadcast_to(floor_present[None], (SLABS, FLOORS, 8)), jnp.broadcast_to(slab_present[:, None, :], (SLABS, FLOORS, 2))], axis=-1)
    target = jax.random.randint(key_target, (), 0, FLOORS)
    full_slab = jax.random.randint(key_slab, (), 1, SLABS - 1)
    halving = jax.random.randint(key_live, (SLABS, FLOORS, 10), 0, 3)
    live = GCAP // jnp.array([1, 2, 4], dtype=jnp.int32)[halving]
    bricks = jnp.arange(FLOORS, dtype=jnp.int32)
    full = jnp.concatenate([jnp.broadcast_to((bricks == target)[None, :, None], (SLABS, FLOORS, 8)), jnp.broadcast_to((slab_ids == full_slab)[:, None, None], (SLABS, FLOORS, 2))], axis=-1)
    live = jnp.where(full, GCAP, live)
    live = jnp.where(present, live, 0)
    bounds = jnp.cumsum(live, axis=-1)
    total = PART_DEV + bounds[..., -1]
    picks = jax.random.randint(key_pick, (SLABS, FLOORS, EDGES_DEV), 0, total[..., None])
    ghost = picks - PART_DEV
    search = jax.vmap(partial(jnp.searchsorted, side='right'))
    block = search(bounds.reshape(SLABS * FLOORS, 10), ghost.reshape(SLABS * FLOORS, EDGES_DEV)).reshape(SLABS, FLOORS, EDGES_DEV)
    block = jnp.clip(block, 0, 9).astype(jnp.int32)
    starts = bounds - live
    start_of = jnp.take_along_axis(starts, block, axis=-1)
    slot = PART_DEV + block * GCAP + ghost - start_of
    value = jnp.where(picks < PART_DEV, picks, slot)
    ends = jnp.where(live > 0, PART_DEV + jnp.arange(10, dtype=jnp.int32)[None, None, :] * GCAP + live - 1, PART_DEV - 1)
    value = value.at[:, :, EDGES_DEV - 1].set(jnp.max(ends, axis=-1))
    return value.reshape(SLABS, FLOORS * EDGES_DEV).astype(jnp.int32)


def plant(values, stream_key, low, largest):
    place = [jax.random.randint(jax.random.fold_in(stream_key, axis), (), 0, length) for axis, length in enumerate(values.shape)]
    widest = values.shape.index(max(values.shape))
    beside = place[:widest] + [(place[widest] + 1) % values.shape[widest]] + place[widest + 1:]
    return values.at[tuple(place)].set(low).at[tuple(beside)].set(largest)


def block_scale(key, dims, cuts, smallest, largest):
    gain, own = 1.0, jax.random.fold_in(key, 6)
    for axis_at, shards_of in cuts:
        steps = jnp.exp(jax.random.uniform(jax.random.fold_in(own, axis_at), (shards_of,), jnp.float32, smallest / len(cuts), largest / len(cuts)))
        gain = gain * jnp.repeat(steps, dims[axis_at] // shards_of).reshape([-1 if axis == axis_at else 1 for axis in range(len(dims))])
    return gain


def bell_draw(own_key, extent, width, most, cuts=(), kind=jnp.bfloat16):
    loudness = block_scale(own_key, extent, cuts, -0.22, 0.18) if cuts else 1.0
    values = jax.random.normal(own_key, extent, jnp.float32) * width * loudness
    return jnp.minimum(jnp.maximum(values, -most), most).astype(kind)


def setup_inputs(seed: int = 0) -> dict:
    arg_keys = jax.random.split(jax.random.key(seed), 16)
    return {
        "latent": bell_draw(arg_keys[0], (SLABS, ROWS, D), 1.0, 6.0, ((0, 8), (1, 16))),
        "edge_geom": bell_draw(arg_keys[1], (SLABS, 3, EDGES), 0.5, 3.0, ((0, 8), (2, 16)), jnp.float32),
        "edge_recv": draw_edge_recv(jax.random.fold_in(arg_keys[15], 71), 0),
        "edge_send": draw_edge_send(jax.random.fold_in(arg_keys[15], 71), 0),
        "ghost_rows": plant(jax.random.randint(arg_keys[4], (SLABS, FLOORS * 10, GCAP), 0, PART_DEV), jax.random.fold_in(arg_keys[4], 1), 0, PART_DEV - 1).astype(jnp.int32),
        "dest": draw_dest(jax.random.fold_in(arg_keys[15], 71), 0),
        "enc_w1": bell_draw(arg_keys[6], (4, D), 4 ** -0.5, 3.0, (), jnp.float32),
        "enc_b1": bell_draw(arg_keys[7], (D,), 0.5, 3.0, (), jnp.float32),
        "enc_w2": bell_draw(arg_keys[8], (D, D), D ** -0.5, 0.5),
        "pe_w1": bell_draw(arg_keys[9], (3, D, D), (3 * D) ** -0.5, 0.3125),
        "pe_w2": bell_draw(arg_keys[10], (D, D), D ** -0.5, 0.5),
        "edge_gain": jnp.clip(1.0 + 0.1 * jax.random.normal(arg_keys[11], (D,), jnp.float32), 0.5, 1.5),
        "pn_w1": bell_draw(arg_keys[12], (2, D, D), (2 * D) ** -0.5, 0.375),
        "pn_w2": bell_draw(arg_keys[13], (D, D), D ** -0.5, 0.5),
        "node_gain": jnp.clip(1.0 + 0.1 * jax.random.normal(arg_keys[14], (D,), jnp.float32), 0.5, 1.5),
    }


STEP_ROW = (-1, -1, -1, 0, 0, 1, 1, 1)
STEP_COL = (-1, 0, 1, -1, 1, -1, 0, 1)
norm_eps = 1e-05

def layer_norm(values):
    centred = values - lax.optimization_barrier(jnp.mean(values, axis=-1, keepdims=True))
    spread = lax.optimization_barrier(jnp.mean(centred * centred, axis=-1, keepdims=True))
    return centred / jnp.sqrt(spread + norm_eps)

def source_brick(brick, direction):
    grid_rows = FLOORS // BCOLS
    source_row = brick // BCOLS - STEP_ROW[direction]
    source_col = brick % BCOLS - STEP_COL[direction]
    present = (source_row >= 0) & (source_row < grid_rows) & (source_col >= 0) & (source_col < BCOLS)
    source = jnp.clip(source_row * BCOLS + source_col, 0, FLOORS - 1).astype(jnp.int32)
    return (source, present)

def reference(latent, edge_geom, edge_recv, edge_send, ghost_rows, dest, enc_w1, enc_b1, enc_w2, pe_w1, pe_w2, edge_gain, pn_w1, pn_w2, node_gain):
    own_all = latent.reshape(SLABS, FLOORS, PART_DEV, D)
    offers = ghost_rows.reshape(SLABS, FLOORS, 10, GCAP)
    geom_all = edge_geom.reshape(SLABS, 3, FLOORS, EDGES_DEV)
    receivers_all = edge_recv.reshape(SLABS, FLOORS, EDGES_DEV)
    senders_all = edge_send.reshape(SLABS, FLOORS, EDGES_DEV)
    targets_all = dest.reshape(SLABS, FLOORS, PART_DEV)
    device_ids = jnp.arange(SLABS * FLOORS, dtype=jnp.int32)

    def one_device(device):
        slab = device // FLOORS
        brick = device % FLOORS
        own = own_all[slab, brick]
        pieces = [own]
        for direction in range(8):
            source, present = source_brick(brick, direction)
            offered = own_all[slab, source][offers[slab, source, direction]]
            pieces.append(jnp.where(present, offered, jnp.zeros_like(offered)))
        upper = jnp.minimum(slab + 1, SLABS - 1)
        offered = own_all[upper, brick][offers[upper, brick, 8]]
        pieces.append(jnp.where(slab + 1 < SLABS, offered, jnp.zeros_like(offered)))
        lower = jnp.maximum(slab - 1, 0)
        offered = own_all[lower, brick][offers[lower, brick, 9]]
        pieces.append(jnp.where(slab >= 1, offered, jnp.zeros_like(offered)))
        extended = jnp.concatenate(pieces, axis=0)
        geom = geom_all[slab, :, brick]
        receivers = receivers_all[slab, brick]
        senders = senders_all[slab, brick]
        length = jnp.sqrt(geom[0] * geom[0] + geom[1] * geom[1] + geom[2] * geom[2])
        first = enc_b1[None, :] + geom[0][:, None] * enc_w1[0][None, :] + geom[1][:, None] * enc_w1[1][None, :] + geom[2][:, None] * enc_w1[2][None, :] + length[:, None] * enc_w1[3][None, :]
        enc_hidden = jax.nn.relu(first).astype(jnp.bfloat16)
        encoded = layer_norm(jnp.dot(enc_hidden, enc_w2, preferred_element_type=jnp.float32))
        encoded_half = encoded.astype(jnp.bfloat16)
        recv_proj = jnp.dot(own, pe_w1[1], preferred_element_type=jnp.float32).astype(jnp.bfloat16)
        send_proj = jnp.dot(extended, pe_w1[2], preferred_element_type=jnp.float32).astype(jnp.bfloat16)
        before = jnp.dot(encoded_half, pe_w1[0], preferred_element_type=jnp.float32) + recv_proj[receivers].astype(jnp.float32) + send_proj[senders].astype(jnp.float32)
        edge_hidden = jax.nn.relu(before).astype(jnp.bfloat16)
        message = encoded + edge_gain * layer_norm(jnp.dot(edge_hidden, pe_w2, preferred_element_type=jnp.float32))
        aggregate = jax.ops.segment_sum(message, receivers, num_segments=PART_DEV)
        node_pre = jnp.dot(own, pn_w1[0], preferred_element_type=jnp.float32) + jnp.dot(aggregate.astype(jnp.bfloat16), pn_w1[1], preferred_element_type=jnp.float32)
        node_hidden = jax.nn.relu(node_pre).astype(jnp.bfloat16)
        updated = own.astype(jnp.float32) + node_gain * layer_norm(jnp.dot(node_hidden, pn_w2, preferred_element_type=jnp.float32))
        return updated.astype(jnp.bfloat16)
    updated_all = lax.map(one_device, device_ids).reshape(SLABS, FLOORS, PART_DEV, D)
    bricks = jnp.arange(FLOORS, dtype=jnp.int32)
    keeping = (targets_all == bricks[None, :, None])[..., None]
    staying = jnp.where(keeping, updated_all, jnp.zeros_like(updated_all)).reshape(SLABS, ROWS, D)

    def arrivals_of(device):
        slab = device // FLOORS
        brick = device % FLOORS
        blocks = []
        for direction in range(8):
            source, present = source_brick(brick, direction)
            moving = (targets_all[slab, source] == brick) & present
            rank = jnp.cumsum(moving.astype(jnp.int32)) - 1
            slot = jnp.where(moving, rank, MCAP)
            block = jnp.zeros((MCAP, D), jnp.bfloat16).at[slot].set(updated_all[slab, source], mode='drop')
            blocks.append(block)
        return jnp.stack(blocks)
    arrivals = lax.map(arrivals_of, device_ids).reshape(SLABS, FLOORS * 8, MCAP, D)
    return (staying, arrivals)
```

```python
import jax
import jax.numpy as jnp
from jax import lax
from jax.experimental import pallas as pl
from jax.experimental.pallas import tpu as pltpu
from jax.sharding import PartitionSpec as P

BCOLS = 4
MCAP = 128
TILE = 128
EDGES = 2048
HALF = 1024
QUART = 512
PARTS = 4096
GHOST = 5120
STEP_ROW = (-1, -1, -1, 0, 0, 1, 1, 1)
STEP_COL = (-1, 0, 1, -1, 1, -1, 0, 1)
EPS = 1e-05
F32 = jnp.float32
BF16 = jnp.bfloat16


def from_behind(value, axis, steps):
    count = lax.axis_size(axis)
    first, last = (max(0, -steps), min(count, count - steps))
    return lax.ppermute(value, axis, [(source, source + steps) for source in range(first, last)])


def dot(a, b):
    return jnp.dot(a, b, preferred_element_type=F32)


def iota(shape, dim):
    return lax.broadcasted_iota(jnp.int32, shape, dim)


def edge_kernel(
    brick_ref,
    geom_ref,
    recv_ref,
    own_ref,
    ext_ref,
    dest_ref,
    send_hbm,
    enc_w1_ref,
    enc_b1_ref,
    enc_w2_ref,
    pe_w1_ref,
    pe_w2_ref,
    edge_gain_ref,
    pn_w1_ref,
    pn_w2_ref,
    node_gain_ref,
    staying_ref,
    outgoing_ref,
    table,
    w_first,
    w_enc,
    w_msg,
    w_mean,
    w_before,
    w_node,
    counts,
    leaving,
    send_a,
    send_b,
    sems,
):
    step = pl.program_id(0)
    steps = pl.num_programs(0)

    def fetch(slot, which, at):
        return pltpu.make_async_copy(
            send_hbm.at[:, pl.ds(at * EDGES + which * HALF, HALF)], slot, sems.at[which]
        )

    @pl.when(step == 0)
    def _():
        fetch(send_a, 0, 0).start()
        fetch(send_b, 1, 0).start()
        w_first[...] = jnp.zeros_like(w_first)
        w_enc[...] = jnp.zeros_like(w_enc)
        w_msg[...] = jnp.zeros_like(w_msg)
        w_mean[...] = jnp.zeros_like(w_mean)
        counts[...] = jnp.zeros_like(counts)
        leaving[...] = jnp.zeros_like(leaving)
        row8 = iota((8, 128), 0)
        weights = jnp.zeros((8, 128), F32)
        for c in range(4):
            weights = jnp.where(row8 == c, enc_w1_ref[c : c + 1, :], weights)
        weights = jnp.where(row8 == 4, enc_b1_ref[0:1, :], weights)
        high = weights.astype(BF16).astype(F32)
        low = weights - high
        pick = jnp.where(row8 == 5, 1.0, 0.0).astype(F32)
        zero = jnp.zeros((8, 128), F32)
        w_first[:, 0:128] = jnp.concatenate([high, high, low, zero], axis=0).astype(BF16)
        w_first[:, 128:256] = jnp.concatenate([pick, zero, zero, zero], axis=0).astype(BF16)

        def centred(ref):
            full = ref[...].astype(F32)
            return (full - jnp.mean(full, axis=1, keepdims=True)).astype(BF16)

        enc = centred(enc_w2_ref)
        msg = centred(pe_w2_ref)
        mean = jnp.full((128, 128), 1.0 / 128, BF16)
        for k in (0, 128):
            w_enc[k : k + 128, k : k + 128] = enc
            w_msg[k : k + 128, k : k + 128] = msg
            w_mean[k : k + 128, k : k + 128] = mean
        w_node[...] = centred(pn_w2_ref)
        w_before[0:128, :] = pe_w1_ref[0]

        @pl.loop(0, (PARTS + GHOST) // 512)
        def _(i):
            at = pl.multiple_of(i * 512, 512)
            block = dot(ext_ref[pl.ds(at, 512), :], pe_w1_ref[2])
            table[pl.ds(at, 512), :] = block.astype(BF16).astype(F32)

    own = own_ref[...]
    w_before[128:256, :] = dot(own, pe_w1_ref[1]).astype(BF16)

    row8 = iota((8, 128), 0)
    lane = iota((HALF, 128), 1).astype(F32)
    rows = iota((TILE, HALF), 0)

    def gathered(slot, first, count):
        blocks = []
        for at in range(first, first + count, 8):
            block = jnp.broadcast_to(table[pl.ds(slot[0, at], 1), :], (8, 128))
            for s in range(1, 8):
                line = jnp.broadcast_to(table[pl.ds(slot[0, at + s], 1), :], (8, 128))
                block = jnp.where(row8 == s, line, block)
            blocks.append(block)
        return jnp.concatenate(blocks, axis=0)

    def normed(values):
        half = values.astype(BF16)
        spread = dot(half * half, w_mean[...])
        return (values * lax.rsqrt(spread + EPS)).astype(BF16)

    def half_tile(which, slot):
        at = which * HALF
        geom = geom_ref[0, :, at : at + HALF]
        local = recv_ref[:, at : at + HALF] - step * TILE
        length = jnp.sqrt(geom[0:1] * geom[0:1] + geom[1:2] * geom[1:2] + geom[2:3] * geom[2:3])
        r8 = iota((8, HALF), 0)
        feats = jnp.where(r8 == 4, 1.0, jnp.zeros((8, HALF), F32))
        for c in range(3):
            feats = jnp.where(r8 == c, geom[c : c + 1], feats)
        feats = jnp.where(r8 == 3, length, feats)
        feats = jnp.where(r8 == 5, local.astype(F32), feats)
        high = feats.astype(BF16).astype(F32)
        low = feats - high
        feats = jnp.concatenate([high, low, high, jnp.zeros_like(high)], axis=0).astype(BF16)
        both = lax.dot_general(
            feats, w_first[...], (((0,), (0,)), ((), ())), preferred_element_type=F32
        )
        hidden = jnp.maximum(both[:, 0:128], 0.0).astype(BF16)
        picks = jnp.where(both[:, 128:256] == lane, 1.0, 0.0).astype(BF16)
        paired = jnp.concatenate([hidden[0:QUART], hidden[QUART:HALF]], axis=1)
        encoded = normed(dot(paired, w_enc[...]))
        left = dot(
            jnp.concatenate([encoded[:, 0:128], picks[0:QUART]], axis=1), w_before[...]
        ) + gathered(slot, 0, QUART)
        right = dot(
            jnp.concatenate([encoded[:, 128:256], picks[QUART:HALF]], axis=1), w_before[...]
        ) + gathered(slot, QUART, QUART)
        paired = jnp.maximum(jnp.concatenate([left, right], axis=1), 0.0).astype(BF16)
        message = normed(dot(paired, w_msg[...]))
        picks_t = jnp.where(rows == local, 1.0, 0.0).astype(BF16)
        joined = jnp.concatenate(
            [
                jnp.concatenate([encoded[:, 0:128], encoded[:, 128:256]], axis=0),
                jnp.concatenate([message[:, 0:128], message[:, 128:256]], axis=0),
            ],
            axis=1,
        )
        return dot(picks_t, joined)

    fetch(send_a, 0, step).wait()
    total = half_tile(0, send_a)

    @pl.when(step + 1 < steps)
    def _():
        fetch(send_a, 0, step + 1).start()

    fetch(send_b, 1, step).wait()
    total += half_tile(1, send_b)

    @pl.when(step + 1 < steps)
    def _():
        fetch(send_b, 1, step + 1).start()

    aggregate = (total[:, 0:128] + edge_gain_ref[0:1, :] * total[:, 128:256]).astype(BF16)
    node = jnp.maximum(dot(own, pn_w1_ref[0]) + dot(aggregate, pn_w1_ref[1]), 0.0).astype(BF16)
    node = dot(node, w_node[...])
    spread = jnp.mean(node * node, axis=1, keepdims=True)
    node = node * lax.rsqrt(spread + EPS)
    updated = (own.astype(F32) + node_gain_ref[0:1, :] * node).astype(BF16)

    brick = brick_ref[0]
    dest = dest_ref[...]
    eye = iota((TILE, TILE), 0) == iota((TILE, TILE), 1)
    stays = jnp.where(eye & (dest == brick), 1.0, 0.0).astype(BF16)
    staying_ref[...] = dot(stays, updated).astype(BF16)
    k8 = iota((8, TILE), 0)
    k9 = jnp.where(k8 >= 4, k8 + 1, k8)
    move_row = dest // BCOLS - brick // BCOLS
    move_col = dest % BCOLS - brick % BCOLS
    code = (move_row + 1) * 3 + move_col + 1
    heads = jnp.where(code == k9, 1.0, 0.0)
    upper = jnp.where(iota((TILE, TILE), 0) <= iota((TILE, TILE), 1), 1.0, 0.0).astype(BF16)
    running = dot(heads.astype(BF16), upper) + counts[...]
    counts[...] += jnp.sum(heads, axis=1, keepdims=True)
    slots = jnp.sum(
        heads * (running + (k8 * MCAP).astype(F32)), axis=0, keepdims=True
    ).astype(jnp.int32) - 1
    chosen = jnp.where(iota((8 * MCAP, TILE), 0) == slots, 1.0, 0.0).astype(BF16)
    leaving[...] += dot(chosen, updated)

    @pl.when(step == steps - 1)
    def _():
        outgoing_ref[...] = leaving[...].astype(BF16)


def edge_call(brick, geom, recv, own, ext, dest, send, params):
    steps = PARTS // TILE
    whole = lambda shape: pl.BlockSpec(shape, lambda i, _: (0,) * len(shape))
    return pl.pallas_call(
        edge_kernel,
        grid_spec=pltpu.PrefetchScalarGridSpec(
            num_scalar_prefetch=1,
            grid=(steps,),
            in_specs=[
                pl.BlockSpec((1, 3, EDGES), lambda i, _: (0, 0, i)),
                pl.BlockSpec((1, EDGES), lambda i, _: (0, i)),
                pl.BlockSpec((TILE, 128), lambda i, _: (i, 0)),
                whole((PARTS + GHOST, 128)),
                pl.BlockSpec((1, TILE), lambda i, _: (0, i)),
                pl.BlockSpec(memory_space=pl.ANY),
                whole((4, 128)),
                whole((1, 128)),
                whole((128, 128)),
                whole((3, 128, 128)),
                whole((128, 128)),
                whole((1, 128)),
                whole((2, 128, 128)),
                whole((128, 128)),
                whole((1, 128)),
            ],
            out_specs=[
                pl.BlockSpec((TILE, 128), lambda i, _: (i, 0)),
                whole((8 * MCAP, 128)),
            ],
            scratch_shapes=[
                pltpu.VMEM((PARTS + GHOST, 128), F32),
                pltpu.VMEM((32, 256), BF16),
                pltpu.VMEM((256, 256), BF16),
                pltpu.VMEM((256, 256), BF16),
                pltpu.VMEM((256, 256), BF16),
                pltpu.VMEM((256, 128), BF16),
                pltpu.VMEM((128, 128), BF16),
                pltpu.VMEM((8, 128), F32),
                pltpu.VMEM((8 * MCAP, 128), F32),
                pltpu.SMEM((1, HALF), jnp.int32),
                pltpu.SMEM((1, HALF), jnp.int32),
                pltpu.SemaphoreType.DMA((2,)),
            ],
        ),
        out_shape=[
            jax.ShapeDtypeStruct((PARTS, 128), BF16),
            jax.ShapeDtypeStruct((8 * MCAP, 128), BF16),
        ],
        compiler_params=pltpu.CompilerParams(vmem_limit_bytes=40 << 20),
        cost_estimate=pl.CostEstimate(
            flops=9_000_000_000, bytes_accessed=6_000_000, transcendentals=1_000_000
        ),
    )(brick, geom, recv, own, ext, dest, send, *params)


def shifted(blocks):
    return jnp.stack(
        [
            from_behind(blocks[k], "floor", STEP_ROW[k] * BCOLS + STEP_COL[k])
            for k in range(8)
        ]
    )


def per_device(
    latent,
    edge_geom,
    edge_recv,
    edge_send,
    ghost_rows,
    dest,
    enc_w1,
    enc_b1,
    enc_w2,
    pe_w1,
    pe_w2,
    edge_gain,
    pn_w1,
    pn_w2,
    node_gain,
):
    own = latent[0]
    brick = lax.axis_index("floor").astype(jnp.int32)
    packets = jnp.take(own, ghost_rows[0].reshape(-1), axis=0).reshape(10, 512, 128)
    floor_blocks = shifted(packets[:8]).reshape(8 * 512, 128)
    above = from_behind(packets[8], "slab", -1)
    below = from_behind(packets[9], "slab", 1)
    ext = jnp.concatenate([own, floor_blocks, above, below], axis=0)
    params = (
        enc_w1,
        enc_b1.reshape(1, 128),
        enc_w2,
        pe_w1,
        pe_w2,
        edge_gain.reshape(1, 128),
        pn_w1,
        pn_w2,
        node_gain.reshape(1, 128),
    )
    staying, outgoing = edge_call(
        brick.reshape(1), edge_geom, edge_recv, own, ext, dest, edge_send, params
    )
    arrived = shifted(outgoing.reshape(8, MCAP, 128))
    return (staying[None], arrived[None])


def solution(mesh):
    in_specs = (
        P("slab", "floor", None),
        P("slab", None, "floor"),
        P("slab", "floor"),
        P("slab", "floor"),
        P("slab", "floor", None),
        P("slab", "floor"),
    ) + (P(),) * 9
    out_specs = (P("slab", "floor", None), P("slab", "floor", None, None))
    return jax.shard_map(
        per_device, mesh=mesh, in_specs=in_specs, out_specs=out_specs, check_vma=False
    )
```

```python
import jax
import jax.numpy as jnp
from jax import lax
from jax.experimental import pallas as pl
from jax.experimental.pallas import tpu as pltpu
from jax.sharding import PartitionSpec as P

BCOLS = 4
MCAP = 128
TILE = 128
EDGES = 2048
HALF = 1024
QUART = 512
PARTS = 4096
GHOST = 5120
STEP_ROW = (-1, -1, -1, 0, 0, 1, 1, 1)
STEP_COL = (-1, 0, 1, -1, 1, -1, 0, 1)
EPS = 1e-05
F32 = jnp.float32
BF16 = jnp.bfloat16


def dot(a, b):
    return jnp.dot(a, b, preferred_element_type=F32)


def iota(shape, dim):
    return lax.broadcasted_iota(jnp.int32, shape, dim)


def edge_kernel(
    brick_ref,
    geom_ref,
    recv_ref,
    own_ref,
    all_ref,
    ghost_ref,
    dest_ref,
    send_hbm,
    enc_w1_ref,
    enc_b1_ref,
    enc_w2_ref,
    pe_w1_ref,
    pe_w2_ref,
    edge_gain_ref,
    pn_w1_ref,
    pn_w2_ref,
    node_gain_ref,
    staying_ref,
    outgoing_ref,
    table,
    w_first,
    w_enc,
    w_msg,
    w_mean,
    w_before,
    w_node,
    counts,
    leaving,
    send_a,
    send_b,
    sems,
):
    step = pl.program_id(0)
    steps = pl.num_programs(0)

    def fetch(slot, which, at):
        return pltpu.make_async_copy(
            send_hbm.at[:, pl.ds(at * EDGES + which * HALF, HALF)], slot, sems.at[which]
        )

    @pl.when(step == 0)
    def _():
        fetch(send_a, 0, 0).start()
        fetch(send_b, 1, 0).start()
        w_first[...] = jnp.zeros_like(w_first)
        w_enc[...] = jnp.zeros_like(w_enc)
        w_msg[...] = jnp.zeros_like(w_msg)
        w_mean[...] = jnp.zeros_like(w_mean)
        counts[...] = jnp.zeros_like(counts)
        leaving[...] = jnp.zeros_like(leaving)
        row8 = iota((8, 128), 0)
        weights = jnp.zeros((8, 128), F32)
        for c in range(4):
            weights = jnp.where(row8 == c, enc_w1_ref[c : c + 1, :], weights)
        weights = jnp.where(row8 == 4, enc_b1_ref[0:1, :], weights)
        high = weights.astype(BF16).astype(F32)
        low = weights - high
        pick = jnp.where(row8 == 5, 1.0, 0.0).astype(F32)
        zero = jnp.zeros((8, 128), F32)
        w_first[:, 0:128] = jnp.concatenate([high, high, low, zero], axis=0).astype(BF16)
        w_first[:, 128:256] = jnp.concatenate([pick, zero, zero, zero], axis=0).astype(BF16)

        def centred(ref):
            full = ref[...].astype(F32)
            return (full - jnp.mean(full, axis=1, keepdims=True)).astype(BF16)

        enc = centred(enc_w2_ref)
        msg = centred(pe_w2_ref)
        mean = jnp.full((128, 128), 1.0 / 128, BF16)
        for k in (0, 128):
            w_enc[k : k + 128, k : k + 128] = enc
            w_msg[k : k + 128, k : k + 128] = msg
            w_mean[k : k + 128, k : k + 128] = mean
        full = pn_w2_ref[...].astype(F32)
        full = full - jnp.mean(full, axis=1, keepdims=True)
        high = full.astype(BF16)
        w_node[0:128, :] = high
        w_node[128:256, :] = (full - high.astype(F32)).astype(BF16)
        w_before[0:128, :] = pe_w1_ref[0]

        @pl.loop(0, PARTS // 512)
        def _(i):
            at = pl.multiple_of(i * 512, 512)
            block = dot(all_ref[pl.ds(at, 512), :], pe_w1_ref[2])
            table[pl.ds(at, 512), :] = block.astype(BF16).astype(F32)

        @pl.loop(0, GHOST // 512)
        def _(i):
            at = pl.multiple_of(i * 512, 512)
            block = dot(ghost_ref[pl.ds(at, 512), :], pe_w1_ref[2])
            table[pl.ds(PARTS + at, 512), :] = block.astype(BF16).astype(F32)

    own = own_ref[...]
    w_before[128:256, :] = dot(own, pe_w1_ref[1]).astype(BF16)

    row8 = iota((8, 128), 0)
    lane = iota((HALF, 128), 1).astype(F32)
    rows = iota((TILE, HALF), 0)

    def gathered(slot, first, count):
        blocks = []
        for at in range(first, first + count, 8):
            block = jnp.broadcast_to(table[pl.ds(slot[0, at], 1), :], (8, 128))
            for s in range(1, 8):
                line = jnp.broadcast_to(table[pl.ds(slot[0, at + s], 1), :], (8, 128))
                block = jnp.where(row8 == s, line, block)
            blocks.append(block)
        return jnp.concatenate(blocks, axis=0)

    def normed(values):
        half = values.astype(BF16)
        spread = dot(half * half, w_mean[...])
        return (values * lax.rsqrt(spread + EPS)).astype(BF16)

    def half_tile(which, slot):
        at = which * HALF
        geom = geom_ref[0, :, at : at + HALF]
        local = recv_ref[:, at : at + HALF] - step * TILE
        length = jnp.sqrt(geom[0:1] * geom[0:1] + geom[1:2] * geom[1:2] + geom[2:3] * geom[2:3])
        r8 = iota((8, HALF), 0)
        feats = jnp.where(r8 == 4, 1.0, jnp.zeros((8, HALF), F32))
        for c in range(3):
            feats = jnp.where(r8 == c, geom[c : c + 1], feats)
        feats = jnp.where(r8 == 3, length, feats)
        feats = jnp.where(r8 == 5, local.astype(F32), feats)
        high = feats.astype(BF16).astype(F32)
        low = feats - high
        feats = jnp.concatenate([high, low, high, jnp.zeros_like(high)], axis=0).astype(BF16)
        both = lax.dot_general(
            feats, w_first[...], (((0,), (0,)), ((), ())), preferred_element_type=F32
        )
        hidden = jnp.maximum(both[:, 0:128], 0.0).astype(BF16)
        picks = jnp.where(both[:, 128:256] == lane, 1.0, 0.0).astype(BF16)
        paired = jnp.concatenate([hidden[0:QUART], hidden[QUART:HALF]], axis=1)
        encoded = normed(dot(paired, w_enc[...]))
        left = dot(
            jnp.concatenate([encoded[:, 0:128], picks[0:QUART]], axis=1), w_before[...]
        ) + gathered(slot, 0, QUART)
        right = dot(
            jnp.concatenate([encoded[:, 128:256], picks[QUART:HALF]], axis=1), w_before[...]
        ) + gathered(slot, QUART, QUART)
        paired = jnp.maximum(jnp.concatenate([left, right], axis=1), 0.0).astype(BF16)
        message = normed(dot(paired, w_msg[...]))
        picks_t = jnp.where(rows == local, 1.0, 0.0).astype(BF16)
        joined = jnp.concatenate(
            [
                jnp.concatenate([encoded[:, 0:128], encoded[:, 128:256]], axis=0),
                jnp.concatenate([message[:, 0:128], message[:, 128:256]], axis=0),
            ],
            axis=1,
        )
        return dot(picks_t, joined)

    fetch(send_a, 0, step).wait()
    total = half_tile(0, send_a)

    @pl.when(step + 1 < steps)
    def _():
        fetch(send_a, 0, step + 1).start()

    fetch(send_b, 1, step).wait()
    total += half_tile(1, send_b)

    @pl.when(step + 1 < steps)
    def _():
        fetch(send_b, 1, step + 1).start()

    aggregate = (total[:, 0:128] + edge_gain_ref[0:1, :] * total[:, 128:256]).astype(BF16)
    node = jnp.maximum(dot(own, pn_w1_ref[0]) + dot(aggregate, pn_w1_ref[1]), 0.0).astype(BF16)
    node = dot(jnp.concatenate([node, node], axis=1), w_node[...])
    spread = jnp.mean(node * node, axis=1, keepdims=True)
    node = node * lax.rsqrt(spread + EPS)
    updated = (own.astype(F32) + node_gain_ref[0:1, :] * node).astype(BF16)

    brick = brick_ref[0]
    dest = dest_ref[...]
    eye = iota((TILE, TILE), 0) == iota((TILE, TILE), 1)
    stays = jnp.where(eye & (dest == brick), 1.0, 0.0).astype(BF16)
    staying_ref[...] = dot(stays, updated).astype(BF16)
    k8 = iota((8, TILE), 0)
    k9 = jnp.where(k8 >= 4, k8 + 1, k8)
    move_row = dest // BCOLS - brick // BCOLS
    move_col = dest % BCOLS - brick % BCOLS
    code = (move_row + 1) * 3 + move_col + 1
    heads = jnp.where(code == k9, 1.0, 0.0)
    upper = jnp.where(iota((TILE, TILE), 0) <= iota((TILE, TILE), 1), 1.0, 0.0).astype(BF16)
    running = dot(heads.astype(BF16), upper) + counts[...]
    counts[...] += jnp.sum(heads, axis=1, keepdims=True)
    slots = jnp.sum(
        heads * (running + (k8 * MCAP).astype(F32)), axis=0, keepdims=True
    ).astype(jnp.int32) - 1
    chosen = jnp.where(iota((8 * MCAP, TILE), 0) == slots, 1.0, 0.0).astype(BF16)
    leaving[...] += dot(chosen, updated)

    @pl.when(step == steps - 1)
    def _():
        outgoing_ref[...] = leaving[...].astype(BF16)


def edge_call(brick, geom, recv, own, ghosts, dest, send, params):
    steps = PARTS // TILE
    whole = lambda shape: pl.BlockSpec(shape, lambda i, _: (0,) * len(shape))
    return pl.pallas_call(
        edge_kernel,
        grid_spec=pltpu.PrefetchScalarGridSpec(
            num_scalar_prefetch=1,
            grid=(steps,),
            in_specs=[
                pl.BlockSpec((1, 3, EDGES), lambda i, _: (0, 0, i)),
                pl.BlockSpec((1, EDGES), lambda i, _: (0, i)),
                pl.BlockSpec((TILE, 128), lambda i, _: (i, 0)),
                whole((PARTS, 128)),
                whole((GHOST, 128)),
                pl.BlockSpec((1, TILE), lambda i, _: (0, i)),
                pl.BlockSpec(memory_space=pl.ANY),
                whole((4, 128)),
                whole((1, 128)),
                whole((128, 128)),
                whole((3, 128, 128)),
                whole((128, 128)),
                whole((1, 128)),
                whole((2, 128, 128)),
                whole((128, 128)),
                whole((1, 128)),
            ],
            out_specs=[
                pl.BlockSpec((TILE, 128), lambda i, _: (i, 0)),
                whole((8 * MCAP, 128)),
            ],
            scratch_shapes=[
                pltpu.VMEM((PARTS + GHOST, 128), F32),
                pltpu.VMEM((32, 256), BF16),
                pltpu.VMEM((256, 256), BF16),
                pltpu.VMEM((256, 256), BF16),
                pltpu.VMEM((256, 256), BF16),
                pltpu.VMEM((256, 128), BF16),
                pltpu.VMEM((256, 128), BF16),
                pltpu.VMEM((8, 128), F32),
                pltpu.VMEM((8 * MCAP, 128), F32),
                pltpu.SMEM((1, HALF), jnp.int32),
                pltpu.SMEM((1, HALF), jnp.int32),
                pltpu.SemaphoreType.DMA((2,)),
            ],
        ),
        out_shape=[
            jax.ShapeDtypeStruct((PARTS, 128), BF16),
            jax.ShapeDtypeStruct((8 * MCAP, 128), BF16),
        ],
        compiler_params=pltpu.CompilerParams(vmem_limit_bytes=40 << 20),
        cost_estimate=pl.CostEstimate(
            flops=9_000_000_000, bytes_accessed=6_000_000, transcendentals=1_000_000
        ),
    )(brick, geom, recv, own, own, ghosts, dest, send, *params)


MESH = pl.DeviceIdType.MESH


def partners(count):
    floor, slab = lax.axis_index("floor"), lax.axis_index("slab")
    row, col = floor // BCOLS, floor % BCOLS
    rows = lax.axis_size("floor") // BCOLS
    slabs = lax.axis_size("slab")

    def inside(r, c):
        return (r >= 0) & (r < rows) & (c >= 0) & (c < BCOLS)

    found = []
    for dr, dc in zip(STEP_ROW, STEP_COL):
        found.append(
            (
                inside(row + dr, col + dc),
                (floor + dr * BCOLS + dc, slab),
                inside(row - dr, col - dc),
            )
        )
    found.append((slab >= 1, (floor, slab - 1), slab + 1 < slabs))
    found.append((slab + 1 < slabs, (floor, slab + 1), slab >= 1))
    return found[:count]


def greet(links):
    barrier = pltpu.get_barrier_semaphore()
    for there, device, _ in links:

        @pl.when(there)
        def _():
            pl.semaphore_signal(barrier, inc=1, device_id=device, device_id_type=MESH)

    peers = 0
    for there, _, _ in links:
        peers = peers + there.astype(jnp.int32)
    pl.semaphore_wait(barrier, peers)


def ghost_kernel(rows_ref, own_ref, ghost_ref, table, packets, send_sems, recv_sems):
    links = partners(10)
    row8 = iota((8, 128), 0)
    ghost_ref[...] = jnp.zeros_like(ghost_ref)

    @pl.loop(0, PARTS // 256)
    def _(i):
        at = pl.multiple_of(i * 256, 256)
        table[pl.ds(at, 256), :] = own_ref[pl.ds(at, 256), :].astype(F32)

    def copy(k, device):
        block = pl.ds(k * 512, 512)
        return pltpu.make_async_remote_copy(
            src_ref=packets.at[block],
            dst_ref=ghost_ref.at[block],
            send_sem=send_sems.at[k],
            recv_sem=recv_sems.at[k],
            device_id=device,
            device_id_type=MESH,
        )

    greet(links)
    for k in (0, 2, 5, 7, 1, 6, 3, 4, 8, 9):
        there, device, _ = links[k]

        @pl.loop(0, 8)
        def _(c):
            at = pl.multiple_of(c * 64, 64)
            blocks = []
            for first in range(0, 64, 8):
                block = None
                for s in range(8):
                    line = jnp.broadcast_to(
                        table[pl.ds(rows_ref[0, k, at + first + s], 1), :], (8, 128)
                    )
                    block = line if s == 0 else jnp.where(row8 == s, line, block)
                blocks.append(block)
            packets[pl.ds(k * 512 + at, 64), :] = jnp.concatenate(blocks, axis=0).astype(BF16)

        @pl.when(there)
        def _():
            copy(k, device).start()

    for k in range(10):
        there, device, comes = links[k]

        @pl.when(there)
        def _():
            copy(k, device).wait_send()

        @pl.when(comes)
        def _():
            copy(k, device).wait_recv()


def ghost_call(ghost_rows, own):
    return pl.pallas_call(
        ghost_kernel,
        in_specs=[
            pl.BlockSpec(memory_space=pltpu.SMEM),
            pl.BlockSpec(memory_space=pltpu.VMEM),
        ],
        out_specs=pl.BlockSpec(memory_space=pltpu.VMEM),
        out_shape=jax.ShapeDtypeStruct((GHOST, 128), BF16),
        scratch_shapes=[
            pltpu.VMEM((PARTS, 128), F32),
            pltpu.VMEM((GHOST, 128), BF16),
            pltpu.SemaphoreType.DMA((10,)),
            pltpu.SemaphoreType.DMA((10,)),
        ],
        compiler_params=pltpu.CompilerParams(
            collective_id=0, has_side_effects=True, vmem_limit_bytes=16 << 20
        ),
    )(ghost_rows, own)


def migrant_kernel(out_ref, arrived_ref, send_sems, recv_sems):
    links = partners(8)
    arrived_ref[...] = jnp.zeros_like(arrived_ref)

    def copy(k, device):
        return pltpu.make_async_remote_copy(
            src_ref=out_ref.at[k],
            dst_ref=arrived_ref.at[k],
            send_sem=send_sems.at[k],
            recv_sem=recv_sems.at[k],
            device_id=device,
            device_id_type=MESH,
        )

    greet(links)
    for k in (0, 2, 5, 7, 1, 6, 3, 4):
        there, device, _ = links[k]

        @pl.when(there)
        def _():
            copy(k, device).start()

    for k in range(8):
        there, device, comes = links[k]

        @pl.when(there)
        def _():
            copy(k, device).wait_send()

        @pl.when(comes)
        def _():
            copy(k, device).wait_recv()


def migrant_call(outgoing):
    return pl.pallas_call(
        migrant_kernel,
        in_specs=[pl.BlockSpec(memory_space=pltpu.VMEM)],
        out_specs=pl.BlockSpec(memory_space=pltpu.VMEM),
        out_shape=jax.ShapeDtypeStruct((8, MCAP, 128), BF16),
        scratch_shapes=[pltpu.SemaphoreType.DMA((8,)), pltpu.SemaphoreType.DMA((8,))],
        compiler_params=pltpu.CompilerParams(collective_id=1, has_side_effects=True),
    )(outgoing)


def per_device(
    latent,
    edge_geom,
    edge_recv,
    edge_send,
    ghost_rows,
    dest,
    enc_w1,
    enc_b1,
    enc_w2,
    pe_w1,
    pe_w2,
    edge_gain,
    pn_w1,
    pn_w2,
    node_gain,
):
    own = latent[0]
    brick = lax.axis_index("floor").astype(jnp.int32)
    ghosts = ghost_call(ghost_rows, own)
    params = (
        enc_w1,
        enc_b1.reshape(1, 128),
        enc_w2,
        pe_w1,
        pe_w2,
        edge_gain.reshape(1, 128),
        pn_w1,
        pn_w2,
        node_gain.reshape(1, 128),
    )
    staying, outgoing = edge_call(
        brick.reshape(1), edge_geom, edge_recv, own, ghosts, dest, edge_send, params
    )
    arrived = migrant_call(outgoing.reshape(8, MCAP, 128))
    return (staying[None], arrived[None])


def solution(mesh):
    in_specs = (
        P("slab", "floor", None),
        P("slab", None, "floor"),
        P("slab", "floor"),
        P("slab", "floor"),
        P("slab", "floor", None),
        P("slab", "floor"),
    ) + (P(),) * 9
    out_specs = (P("slab", "floor", None), P("slab", "floor", None, None))
    return jax.shard_map(
        per_device, mesh=mesh, in_specs=in_specs, out_specs=out_specs, check_vma=False
    )
```

```python
import jax
import jax.numpy as jnp
from jax import lax
from jax.experimental import pallas as pl
from jax.experimental.pallas import tpu as pltpu
from jax.sharding import PartitionSpec as P

BCOLS = 4
MCAP = 128
TILE = 128
TILES = 32
CHUNK = 1024
PAIR = 512
PER = 2048 // CHUNK
BLOCK = 512
PARTS = 4096
GHOST = 5120
STEP_ROW = (-1, -1, -1, 0, 0, 1, 1, 1)
STEP_COL = (-1, 0, 1, -1, 1, -1, 0, 1)
EPS = 1e-05
F32 = jnp.float32
BF16 = jnp.bfloat16


def dot(a, b):
    return jnp.dot(a, b, preferred_element_type=F32)


def iota(shape, dim):
    return lax.broadcasted_iota(jnp.int32, shape, dim)


def edge_kernel(
    brick_ref,
    geom_ref,
    recv_ref,
    own_ref,
    ghost_ref,
    dest_ref,
    send_hbm,
    enc_w1_ref,
    enc_b1_ref,
    enc_w2_ref,
    pe_w1_ref,
    pe_w2_ref,
    edge_gain_ref,
    pn_w1_ref,
    pn_w2_ref,
    node_gain_ref,
    staying_ref,
    outgoing_ref,
    table,
    recv_proj,
    summed,
    w_first,
    w_enc,
    w_msg,
    w_node,
    hidden,
    picked,
    picked_t,
    encoded,
    mixed,
    message,
    counts,
    updated,
    leaving,
    send_0,
    send_1,
    send_2,
    send_3,
    sems,
):
    slots = (send_0, send_1, send_2, send_3)
    chunks = TILES * PER

    def fetch(slot, chunk):
        at = jnp.clip(chunk, 0, chunks - 1) * CHUNK
        return pltpu.make_async_copy(
            send_hbm.at[:, pl.ds(pl.multiple_of(at, CHUNK), CHUNK)], slots[slot], sems.at[slot]
        )

    for ahead in (-2, -1, 0):
        fetch(ahead % 4, ahead).start()

    w_first[...] = jnp.zeros_like(w_first)
    w_enc[...] = jnp.zeros_like(w_enc)
    w_msg[...] = jnp.zeros_like(w_msg)
    counts[...] = jnp.zeros_like(counts)
    leaving[...] = jnp.zeros_like(leaving)
    row8 = iota((8, 128), 0)
    weights = jnp.zeros((8, 128), F32)
    for c in range(4):
        weights = jnp.where(row8 == c, enc_w1_ref[c : c + 1, :], weights)
    weights = jnp.where(row8 == 4, enc_b1_ref[0:1, :], weights)
    high = weights.astype(BF16).astype(F32)
    weights = jnp.concatenate(
        [high, high, weights - high, jnp.zeros((8, 128), F32)], axis=0
    ).astype(BF16)
    w_first[0:32, 0:128] = weights
    w_first[32:64, 128:256] = weights

    def centred(ref):
        full = ref[...].astype(F32)
        return full - jnp.mean(full, axis=1, keepdims=True)

    enc = centred(enc_w2_ref).astype(BF16)
    msg = centred(pe_w2_ref).astype(BF16)
    for k in (0, 128):
        w_enc[k : k + 128, k : k + 128] = enc
        w_msg[k : k + 128, k : k + 128] = msg
    full = centred(pn_w2_ref)
    high = full.astype(BF16)
    w_node[0:128, :] = high
    w_node[128:256, :] = (full - high.astype(F32)).astype(BF16)

    w_both = jnp.concatenate([pe_w1_ref[2], pe_w1_ref[1]], axis=1)

    @pl.loop(0, PARTS // 1024)
    def _(i):
        at = pl.multiple_of(i * 1024, 1024)
        block = dot(own_ref[pl.ds(at, 1024), :], w_both).astype(BF16)
        table[pl.ds(at, 1024), :] = block[:, 0:128].astype(F32)
        recv_proj[pl.ds(at, 1024), :] = block[:, 128:256]

    @pl.loop(0, GHOST // 1024)
    def _(i):
        at = pl.multiple_of(i * 1024, 1024)
        block = dot(ghost_ref[pl.ds(at, 1024), :], pe_w1_ref[2])
        table[pl.ds(PARTS + at, 1024), :] = block.astype(BF16).astype(F32)

    rows = iota((TILE, CHUNK), 0)
    r8 = iota((8, CHUNK), 0)

    def gathered(slot, first, count):
        blocks = []
        for at in range(first, first + count, 8):
            block = jnp.broadcast_to(table[pl.ds(slot[0, at], 1), :], (8, 128))
            for s in range(1, 8):
                line = jnp.broadcast_to(table[pl.ds(slot[0, at + s], 1), :], (8, 128))
                block = jnp.where(row8 == s, line, block)
            blocks.append(block)
        return jnp.concatenate(blocks, axis=0)

    def normed(values):
        spread = jnp.sum(values * values, axis=1, keepdims=True) * (1.0 / 128)
        return (values * lax.rsqrt(spread + EPS)).astype(BF16)

    def first_layer(chunk, tile, q):
        at = pl.multiple_of(chunk * CHUNK, CHUNK)
        geom = geom_ref[0, :, pl.ds(at, CHUNK)]
        local = recv_ref[:, pl.ds(at, CHUNK)] - tile * TILE
        length = jnp.sqrt(geom[0:1] * geom[0:1] + geom[1:2] * geom[1:2] + geom[2:3] * geom[2:3])
        feats = jnp.where(r8 == 4, 1.0, jnp.zeros((8, CHUNK), F32))
        for c in range(3):
            feats = jnp.where(r8 == c, geom[c : c + 1], feats)
        feats = jnp.where(r8 == 3, length, feats)
        high = feats.astype(BF16).astype(F32)
        low = feats - high
        feats = jnp.concatenate([high, low, high, jnp.zeros_like(high)], axis=0)
        feats = jnp.concatenate([feats[:, 0:PAIR], feats[:, PAIR:CHUNK]], axis=0).astype(BF16)
        out = lax.dot_general(
            feats, w_first[...], (((0,), (0,)), ((), ())), preferred_element_type=F32
        )
        hidden[...] = jnp.maximum(out, 0.0).astype(BF16)
        picks_t = jnp.where(rows == local, 1.0, 0.0).astype(BF16)
        picked_t[q] = picks_t
        picked[q % 2] = picks_t.T

    def encode(q):
        out = dot(hidden[...], w_enc[...])
        encoded[q, :, 0:128] = normed(out[:, 0:128])
        encoded[q, :, 128:256] = normed(out[:, 128:256])

    def mix(tile, q):
        at = pl.multiple_of(tile * TILE, TILE)
        w_mix = jnp.concatenate([pe_w1_ref[0], recv_proj[pl.ds(at, TILE), :]], axis=0)
        for side in range(2):
            lanes = slice(side * 128, side * 128 + 128)
            lhs = jnp.concatenate(
                [encoded[q, :, lanes], picked[q % 2, side * PAIR : side * PAIR + PAIR, :]], axis=1
            )
            out = dot(lhs, w_mix) + gathered(slots[q], side * PAIR, PAIR)
            mixed[:, lanes] = jnp.maximum(out, 0.0).astype(BF16)

    def messages():
        out = dot(mixed[...], w_msg[...])
        message[:, 0:128] = normed(out[:, 0:128])
        message[:, 128:256] = normed(out[:, 128:256])

    def gather_up(tile, q, first):
        out = None
        for side in range(2):
            lanes = slice(side * 128, side * 128 + 128)
            rhs = jnp.concatenate([encoded[q, :, lanes], message[:, lanes]], axis=1)
            part = dot(picked_t[q, :, side * PAIR : side * PAIR + PAIR], rhs)
            out = part if side == 0 else out + part
        at = pl.multiple_of(tile * TILE, TILE)
        if first:
            summed[pl.ds(at, TILE), :] = out
        else:
            summed[pl.ds(at, TILE), :] += out

    def body(t, q, final=False):
        chunk = t * 4 + q

        def tile(back):
            at = t * (4 // PER) + (q - back) // PER
            return at if final else jnp.maximum(at, 0)

        live = lambda back: not final or q < back
        if live(2):
            fetch((q - 2) % 4, chunk - 2).wait()
        if live(-1):
            fetch((q + 1) % 4, chunk + 1).start()
        gather_up(tile(4), q, q % PER == 0)
        if live(3):
            messages()
        if live(2):
            mix(tile(2), (q - 2) % 4)
        if live(1):
            encode((q - 1) % 4)
        if live(0):
            first_layer(chunk, tile(0), q)

    @pl.loop(0, chunks // 4)
    def _(t):
        for q in range(4):
            body(t, q)

    for q in range(4):
        body(chunks // 4, q, True)
    fetch(0, chunks).wait()

    brick = brick_ref[0]
    k8 = iota((8, TILE), 0)
    k9 = jnp.where(k8 >= 4, k8 + 1, k8)
    diagonal = iota((TILE, TILE), 0) == iota((TILE, TILE), 1)
    upper = jnp.where(iota((TILE, TILE), 0) <= iota((TILE, TILE), 1), 1.0, 0.0).astype(BF16)

    w_both = jnp.concatenate([pn_w1_ref[0], pn_w1_ref[1]], axis=0)

    def node(b):
        at = pl.multiple_of(b * BLOCK, BLOCK)
        own = own_ref[pl.ds(at, BLOCK), :]
        total = summed[pl.ds(at, BLOCK), :]
        aggregate = (total[:, 0:128] + edge_gain_ref[0:1, :] * total[:, 128:256]).astype(BF16)
        out = dot(jnp.concatenate([own, aggregate], axis=1), w_both)
        out = jnp.maximum(out, 0.0).astype(BF16)
        out = dot(jnp.concatenate([out, out], axis=1), w_node[...])
        spread = jnp.sum(out * out, axis=1, keepdims=True) * (1.0 / 128)
        out = out * lax.rsqrt(spread + EPS)
        fresh = (own.astype(F32) + node_gain_ref[0:1, :] * out).astype(BF16)
        updated[pl.ds(at, BLOCK), :] = fresh
        for i in range(0, BLOCK, TILE):
            dest = dest_ref[:, pl.ds(at + i, TILE)]
            stays = jnp.where(diagonal & (dest == brick), 1.0, 0.0).astype(BF16)
            staying_ref[pl.ds(at + i, TILE), :] = dot(stays, fresh[i : i + TILE]).astype(BF16)

    def pack(b):
        at = pl.multiple_of(b * BLOCK, BLOCK)
        places = []
        seen = counts[...]
        for i in range(0, BLOCK, TILE):
            dest = dest_ref[:, pl.ds(at + i, TILE)]
            move_row = dest // BCOLS - brick // BCOLS
            move_col = dest % BCOLS - brick % BCOLS
            code = (move_row + 1) * 3 + move_col + 1
            heads = jnp.where(code == k9, 1.0, 0.0)
            running = dot(heads.astype(BF16), upper) + seen
            seen = seen + jnp.sum(heads, axis=1, keepdims=True)
            places.append(
                jnp.sum(
                    heads * (running + (k8 * MCAP).astype(F32)), axis=0, keepdims=True
                ).astype(jnp.int32) - 1
            )
        counts[...] = seen
        place = jnp.concatenate(places, axis=1)
        for k in range(0, 8 * MCAP, 256):
            chosen = jnp.where(iota((256, BLOCK), 0) + k == place, 1.0, 0.0).astype(BF16)
            leaving[k : k + 256, :] += dot(chosen, updated[pl.ds(at, BLOCK), :])

    node(0)

    @pl.loop(1, PARTS // BLOCK)
    def _(b):
        pack(b - 1)
        node(b)

    pack(PARTS // BLOCK - 1)
    outgoing_ref[...] = leaving[...].astype(BF16)


def edge_call(brick, geom, recv, own, ghosts, dest, send, params):
    vmem = pl.BlockSpec(memory_space=pltpu.VMEM)
    return pl.pallas_call(
        edge_kernel,
        in_specs=[pl.BlockSpec(memory_space=pltpu.SMEM)]
        + [vmem] * 5
        + [pl.BlockSpec(memory_space=pl.ANY)]
        + [vmem] * 9,
        out_specs=[vmem, vmem],
        out_shape=[
            jax.ShapeDtypeStruct((PARTS, 128), BF16),
            jax.ShapeDtypeStruct((8 * MCAP, 128), BF16),
        ],
        scratch_shapes=[
            pltpu.VMEM((PARTS + GHOST, 128), F32),
            pltpu.VMEM((PARTS, 128), BF16),
            pltpu.VMEM((PARTS, 256), F32),
            pltpu.VMEM((64, 256), BF16),
            pltpu.VMEM((256, 256), BF16),
            pltpu.VMEM((256, 256), BF16),
            pltpu.VMEM((256, 128), BF16),
            pltpu.VMEM((PAIR, 256), BF16),
            pltpu.VMEM((2, CHUNK, 128), BF16),
            pltpu.VMEM((4, TILE, CHUNK), BF16),
            pltpu.VMEM((4, PAIR, 256), BF16),
            pltpu.VMEM((PAIR, 256), BF16),
            pltpu.VMEM((PAIR, 256), BF16),
            pltpu.VMEM((8, 128), F32),
            pltpu.VMEM((PARTS, 128), BF16),
            pltpu.VMEM((8 * MCAP, 128), F32),
        ]
        + [pltpu.SMEM((1, CHUNK), jnp.int32)] * 4
        + [pltpu.SemaphoreType.DMA((4,))],
        compiler_params=pltpu.CompilerParams(vmem_limit_bytes=40 << 20),
        cost_estimate=pl.CostEstimate(
            flops=9_000_000_000, bytes_accessed=6_000_000, transcendentals=1_000_000
        ),
    )(brick, geom, recv, own, ghosts, dest, send, *params)


MESH = pl.DeviceIdType.MESH


def partners(count):
    floor, slab = lax.axis_index("floor"), lax.axis_index("slab")
    row, col = floor // BCOLS, floor % BCOLS
    rows = lax.axis_size("floor") // BCOLS
    slabs = lax.axis_size("slab")

    def inside(r, c):
        return (r >= 0) & (r < rows) & (c >= 0) & (c < BCOLS)

    found = []
    for dr, dc in zip(STEP_ROW, STEP_COL):
        found.append(
            (
                inside(row + dr, col + dc),
                (floor + dr * BCOLS + dc, slab),
                inside(row - dr, col - dc),
            )
        )
    found.append((slab >= 1, (floor, slab - 1), slab + 1 < slabs))
    found.append((slab + 1 < slabs, (floor, slab + 1), slab >= 1))
    return found[:count]


def greet(links):
    barrier = pltpu.get_barrier_semaphore()
    for there, device, _ in links:

        @pl.when(there)
        def _():
            pl.semaphore_signal(barrier, inc=1, device_id=device, device_id_type=MESH)

    peers = 0
    for there, _, _ in links:
        peers = peers + there.astype(jnp.int32)
    pl.semaphore_wait(barrier, peers)


def ghost_kernel(rows_ref, own_ref, ghost_ref, table, packets, send_sems, recv_sems):
    links = partners(10)
    row8 = iota((8, 128), 0)
    ghost_ref[...] = jnp.zeros_like(ghost_ref)

    @pl.loop(0, PARTS // 256)
    def _(i):
        at = pl.multiple_of(i * 256, 256)
        table[pl.ds(at, 256), :] = own_ref[pl.ds(at, 256), :].astype(F32)

    def copy(k, device):
        block = pl.ds(k * 512, 512)
        return pltpu.make_async_remote_copy(
            src_ref=packets.at[block],
            dst_ref=ghost_ref.at[block],
            send_sem=send_sems.at[k],
            recv_sem=recv_sems.at[k],
            device_id=device,
            device_id_type=MESH,
        )

    greet(links)
    for k in (0, 2, 5, 7, 1, 6, 3, 4, 8, 9):
        there, device, _ = links[k]

        @pl.loop(0, 8)
        def _(c):
            at = pl.multiple_of(c * 64, 64)
            blocks = []
            for first in range(0, 64, 8):
                block = None
                for s in range(8):
                    line = jnp.broadcast_to(
                        table[pl.ds(rows_ref[0, k, at + first + s], 1), :], (8, 128)
                    )
                    block = line if s == 0 else jnp.where(row8 == s, line, block)
                blocks.append(block)
            packets[pl.ds(k * 512 + at, 64), :] = jnp.concatenate(blocks, axis=0).astype(BF16)

        @pl.when(there)
        def _():
            copy(k, device).start()

    for k in range(10):
        there, device, comes = links[k]

        @pl.when(there)
        def _():
            copy(k, device).wait_send()

        @pl.when(comes)
        def _():
            copy(k, device).wait_recv()


def ghost_call(ghost_rows, own):
    return pl.pallas_call(
        ghost_kernel,
        in_specs=[
            pl.BlockSpec(memory_space=pltpu.SMEM),
            pl.BlockSpec(memory_space=pltpu.VMEM),
        ],
        out_specs=pl.BlockSpec(memory_space=pltpu.VMEM),
        out_shape=jax.ShapeDtypeStruct((GHOST, 128), BF16),
        scratch_shapes=[
            pltpu.VMEM((PARTS, 128), F32),
            pltpu.VMEM((GHOST, 128), BF16),
            pltpu.SemaphoreType.DMA((10,)),
            pltpu.SemaphoreType.DMA((10,)),
        ],
        compiler_params=pltpu.CompilerParams(
            collective_id=0, has_side_effects=True, vmem_limit_bytes=16 << 20
        ),
    )(ghost_rows, own)


def migrant_kernel(out_ref, arrived_ref, send_sems, recv_sems):
    links = partners(8)
    arrived_ref[...] = jnp.zeros_like(arrived_ref)

    def copy(k, device):
        return pltpu.make_async_remote_copy(
            src_ref=out_ref.at[k],
            dst_ref=arrived_ref.at[k],
            send_sem=send_sems.at[k],
            recv_sem=recv_sems.at[k],
            device_id=device,
            device_id_type=MESH,
        )

    greet(links)
    for k in (0, 2, 5, 7, 1, 6, 3, 4):
        there, device, _ = links[k]

        @pl.when(there)
        def _():
            copy(k, device).start()

    for k in range(8):
        there, device, comes = links[k]

        @pl.when(there)
        def _():
            copy(k, device).wait_send()

        @pl.when(comes)
        def _():
            copy(k, device).wait_recv()


def migrant_call(outgoing):
    return pl.pallas_call(
        migrant_kernel,
        in_specs=[pl.BlockSpec(memory_space=pltpu.VMEM)],
        out_specs=pl.BlockSpec(memory_space=pltpu.VMEM),
        out_shape=jax.ShapeDtypeStruct((8, MCAP, 128), BF16),
        scratch_shapes=[pltpu.SemaphoreType.DMA((8,)), pltpu.SemaphoreType.DMA((8,))],
        compiler_params=pltpu.CompilerParams(collective_id=1, has_side_effects=True),
    )(outgoing)


def per_device(
    latent,
    edge_geom,
    edge_recv,
    edge_send,
    ghost_rows,
    dest,
    enc_w1,
    enc_b1,
    enc_w2,
    pe_w1,
    pe_w2,
    edge_gain,
    pn_w1,
    pn_w2,
    node_gain,
):
    own = latent[0]
    brick = lax.axis_index("floor").astype(jnp.int32)
    ghosts = ghost_call(ghost_rows, own)
    params = (
        enc_w1,
        enc_b1.reshape(1, 128),
        enc_w2,
        pe_w1,
        pe_w2,
        edge_gain.reshape(1, 128),
        pn_w1,
        pn_w2,
        node_gain.reshape(1, 128),
    )
    staying, outgoing = edge_call(
        brick.reshape(1), edge_geom, edge_recv, own, ghosts, dest, edge_send, params
    )
    arrived = migrant_call(outgoing.reshape(8, MCAP, 128))
    return (staying[None], arrived[None])


def solution(mesh):
    in_specs = (
        P("slab", "floor", None),
        P("slab", None, "floor"),
        P("slab", "floor"),
        P("slab", "floor"),
        P("slab", "floor", None),
        P("slab", "floor"),
    ) + (P(),) * 9
    out_specs = (P("slab", "floor", None), P("slab", "floor", None, None))
    return jax.shard_map(
        per_device, mesh=mesh, in_specs=in_specs, out_specs=out_specs, check_vma=False
    )
```

```python
import jax
import jax.numpy as jnp
from jax import lax
from jax.experimental import pallas as pl
from jax.experimental.pallas import tpu as pltpu
from jax.sharding import PartitionSpec as P

BCOLS = 4
MCAP = 128
TILE = 128
TILES = 32
CHUNK = 1024
PAIR = 512
PER = 2048 // CHUNK
BLOCK = 1024
PARTS = 4096
GHOST = 5120
STEP_ROW = (-1, -1, -1, 0, 0, 1, 1, 1)
STEP_COL = (-1, 0, 1, -1, 1, -1, 0, 1)
EPS = 1e-05
F32 = jnp.float32
BF16 = jnp.bfloat16


def dot(a, b):
    return jnp.dot(a, b, preferred_element_type=F32)


def iota(shape, dim):
    return lax.broadcasted_iota(jnp.int32, shape, dim)


def edge_kernel(
    brick_ref,
    geom_ref,
    recv_ref,
    own_ref,
    ghost_ref,
    dest_ref,
    send_hbm,
    enc_w1_ref,
    enc_b1_ref,
    enc_w2_ref,
    pe_w1_ref,
    pe_w2_ref,
    edge_gain_ref,
    pn_w1_ref,
    pn_w2_ref,
    node_gain_ref,
    staying_ref,
    outgoing_ref,
    table,
    recv_proj,
    summed,
    w_first,
    w_enc,
    w_msg,
    w_node,
    w_mean,
    hidden,
    picked,
    picked_t,
    encoded,
    mixed,
    message,
    counts,
    updated,
    leaving,
    send_0,
    send_1,
    send_2,
    send_3,
    sems,
):
    slots = (send_0, send_1, send_2, send_3)
    chunks = TILES * PER

    def fetch(slot, chunk):
        at = jnp.clip(chunk, 0, chunks - 1) * CHUNK
        return pltpu.make_async_copy(
            send_hbm.at[:, pl.ds(pl.multiple_of(at, CHUNK), CHUNK)], slots[slot], sems.at[slot]
        )

    for ahead in (-2, -1, 0):
        fetch(ahead % 4, ahead).start()

    w_first[...] = jnp.zeros_like(w_first)
    w_enc[...] = jnp.zeros_like(w_enc)
    w_mean[...] = jnp.zeros_like(w_mean)
    w_msg[...] = jnp.zeros_like(w_msg)
    counts[...] = jnp.zeros_like(counts)
    leaving[...] = jnp.zeros_like(leaving)
    row8 = iota((8, 128), 0)
    weights = jnp.zeros((8, 128), F32)
    for c in range(4):
        weights = jnp.where(row8 == c, enc_w1_ref[c : c + 1, :], weights)
    weights = jnp.where(row8 == 4, enc_b1_ref[0:1, :], weights)
    high = weights.astype(BF16).astype(F32)
    weights = jnp.concatenate(
        [high, high, weights - high, jnp.zeros((8, 128), F32)], axis=0
    ).astype(BF16)
    w_first[0:32, 0:128] = weights
    w_first[32:64, 128:256] = weights

    def centred(ref):
        full = ref[...].astype(F32)
        return full - jnp.mean(full, axis=1, keepdims=True)

    enc = centred(enc_w2_ref).astype(BF16)
    msg = centred(pe_w2_ref).astype(BF16)
    for k in (0, 128):
        w_enc[k : k + 128, k : k + 128] = enc
        w_mean[k : k + 128, k : k + 128] = jnp.full((128, 128), 1.0 / 128, BF16)
        w_msg[k : k + 128, k : k + 128] = msg
    full = centred(pn_w2_ref)
    high = full.astype(BF16)
    w_node[0:128, :] = high
    w_node[128:256, :] = (full - high.astype(F32)).astype(BF16)

    w_both = jnp.concatenate([pe_w1_ref[2], pe_w1_ref[1]], axis=1)

    @pl.loop(0, PARTS // 1024, unroll=2)
    def _(i):
        at = pl.multiple_of(i * 1024, 1024)
        block = dot(own_ref[pl.ds(at, 1024), :], w_both).astype(BF16)
        table[pl.ds(at, 1024), :] = block[:, 0:128].astype(F32)
        recv_proj[pl.ds(at, 1024), :] = block[:, 128:256]

    @pl.loop(0, GHOST // 1024, unroll=True)
    def _(i):
        at = pl.multiple_of(i * 1024, 1024)
        block = dot(ghost_ref[pl.ds(at, 1024), :], pe_w1_ref[2])
        table[pl.ds(PARTS + at, 1024), :] = block.astype(BF16).astype(F32)

    rows = iota((TILE, CHUNK), 0)
    r8 = iota((8, CHUNK), 0)

    def gathered(slot, first, count):
        blocks = []
        for at in range(first, first + count, 8):
            block = jnp.broadcast_to(table[pl.ds(slot[0, at], 1), :], (8, 128))
            for s in range(1, 8):
                line = jnp.broadcast_to(table[pl.ds(slot[0, at + s], 1), :], (8, 128))
                block = jnp.where(row8 == s, line, block)
            blocks.append(block)
        return jnp.concatenate(blocks, axis=0)

    def normed(values):
        spread = jnp.sum(values * values, axis=1, keepdims=True) * (1.0 / 128)
        return (values * lax.rsqrt(spread + EPS)).astype(BF16)

    def normed_pair(values):
        half = values.astype(BF16)
        spread = dot(half * half, w_mean[...])
        return (values * lax.rsqrt(spread + EPS)).astype(BF16)

    def first_layer(chunk, tile, q):
        at = pl.multiple_of(chunk * CHUNK, CHUNK)
        geom = geom_ref[0, :, pl.ds(at, CHUNK)]
        local = recv_ref[:, pl.ds(at, CHUNK)] - tile * TILE
        length = jnp.sqrt(geom[0:1] * geom[0:1] + geom[1:2] * geom[1:2] + geom[2:3] * geom[2:3])
        feats = jnp.where(r8 == 4, 1.0, jnp.zeros((8, CHUNK), F32))
        for c in range(3):
            feats = jnp.where(r8 == c, geom[c : c + 1], feats)
        feats = jnp.where(r8 == 3, length, feats)
        high = feats.astype(BF16).astype(F32)
        low = feats - high
        feats = jnp.concatenate([high, low, high, jnp.zeros_like(high)], axis=0)
        feats = jnp.concatenate([feats[:, 0:PAIR], feats[:, PAIR:CHUNK]], axis=0).astype(BF16)
        out = lax.dot_general(
            feats, w_first[...], (((0,), (0,)), ((), ())), preferred_element_type=F32
        )
        hidden[...] = jnp.maximum(out, 0.0).astype(BF16)
        picks_t = jnp.where(rows == local, 1.0, 0.0).astype(BF16)
        picked_t[q] = picks_t
        picked[q % 2] = picks_t.T

    def encode(q):
        out = dot(hidden[...], w_enc[...])
        encoded[q] = normed_pair(out)

    def mix(tile, q):
        at = pl.multiple_of(tile * TILE, TILE)
        w_mix = jnp.concatenate([pe_w1_ref[0], recv_proj[pl.ds(at, TILE), :]], axis=0)
        for side in range(2):
            lanes = slice(side * 128, side * 128 + 128)
            lhs = jnp.concatenate(
                [encoded[q, :, lanes], picked[q % 2, side * PAIR : side * PAIR + PAIR, :]], axis=1
            )
            out = dot(lhs, w_mix) + gathered(slots[q], side * PAIR, PAIR)
            mixed[:, lanes] = jnp.maximum(out, 0.0).astype(BF16)

    def messages():
        out = dot(mixed[...], w_msg[...])
        message[...] = normed_pair(out)

    def gather_up(tile, q, first):
        out = None
        for side in range(2):
            lanes = slice(side * 128, side * 128 + 128)
            rhs = jnp.concatenate([encoded[q, :, lanes], message[:, lanes]], axis=1)
            part = dot(picked_t[q, :, side * PAIR : side * PAIR + PAIR], rhs)
            out = part if side == 0 else out + part
        at = pl.multiple_of(tile * TILE, TILE)
        if first:
            summed[pl.ds(at, TILE), :] = out
        else:
            summed[pl.ds(at, TILE), :] += out

    def body(t, q, final=False):
        chunk = t * 4 + q

        def tile(back):
            at = t * (4 // PER) + (q - back) // PER
            return at if final else jnp.maximum(at, 0)

        live = lambda back: not final or q < back
        if live(2):
            fetch((q - 2) % 4, chunk - 2).wait()
        if live(-1):
            fetch((q + 1) % 4, chunk + 1).start()
        gather_up(tile(4), q, q % PER == 0)
        if live(3):
            messages()
        if live(2):
            mix(tile(2), (q - 2) % 4)
        if live(1):
            encode((q - 1) % 4)
        if live(0):
            first_layer(chunk, tile(0), q)

    @pl.loop(0, chunks // 4)
    def _(t):
        for q in range(4):
            body(t, q)

    for q in range(4):
        body(chunks // 4, q, True)
    fetch(0, chunks).wait()

    brick = brick_ref[0]
    k8 = iota((8, TILE), 0)
    k9 = jnp.where(k8 >= 4, k8 + 1, k8)
    diagonal = iota((TILE, TILE), 0) == iota((TILE, TILE), 1)
    upper = jnp.where(iota((TILE, TILE), 0) <= iota((TILE, TILE), 1), 1.0, 0.0).astype(BF16)

    w_both = jnp.concatenate([pn_w1_ref[0], pn_w1_ref[1]], axis=0)

    def node(b):
        at = pl.multiple_of(b * BLOCK, BLOCK)
        own = own_ref[pl.ds(at, BLOCK), :]
        total = summed[pl.ds(at, BLOCK), :]
        aggregate = (total[:, 0:128] + edge_gain_ref[0:1, :] * total[:, 128:256]).astype(BF16)
        out = dot(jnp.concatenate([own, aggregate], axis=1), w_both)
        out = jnp.maximum(out, 0.0).astype(BF16)
        out = dot(jnp.concatenate([out, out], axis=1), w_node[...])
        spread = jnp.sum(out * out, axis=1, keepdims=True) * (1.0 / 128)
        out = out * lax.rsqrt(spread + EPS)
        fresh = (own.astype(F32) + node_gain_ref[0:1, :] * out).astype(BF16)
        updated[pl.ds(at, BLOCK), :] = fresh
        for i in range(0, BLOCK, TILE):
            dest = dest_ref[:, pl.ds(at + i, TILE)]
            stays = jnp.where(diagonal & (dest == brick), 1.0, 0.0).astype(BF16)
            staying_ref[pl.ds(at + i, TILE), :] = dot(stays, fresh[i : i + TILE]).astype(BF16)

    def pack(b):
        at = pl.multiple_of(b * BLOCK, BLOCK)
        places = []
        seen = counts[...]
        for i in range(0, BLOCK, TILE):
            dest = dest_ref[:, pl.ds(at + i, TILE)]
            move_row = dest // BCOLS - brick // BCOLS
            move_col = dest % BCOLS - brick % BCOLS
            code = (move_row + 1) * 3 + move_col + 1
            heads = jnp.where(code == k9, 1.0, 0.0)
            running = dot(heads.astype(BF16), upper) + seen
            seen = seen + jnp.sum(heads, axis=1, keepdims=True)
            places.append(
                jnp.sum(
                    heads * (running + (k8 * MCAP).astype(F32)), axis=0, keepdims=True
                ).astype(jnp.int32) - 1
            )
        counts[...] = seen
        place = jnp.concatenate(places, axis=1)
        for k in range(0, 8 * MCAP, 256):
            chosen = jnp.where(iota((256, BLOCK), 0) + k == place, 1.0, 0.0).astype(BF16)
            leaving[k : k + 256, :] += dot(chosen, updated[pl.ds(at, BLOCK), :])

    node(0)

    @pl.loop(1, PARTS // BLOCK)
    def _(b):
        pack(b - 1)
        node(b)

    pack(PARTS // BLOCK - 1)
    outgoing_ref[...] = leaving[...].astype(BF16)


def edge_call(brick, geom, recv, own, ghosts, dest, send, params):
    vmem = pl.BlockSpec(memory_space=pltpu.VMEM)
    return pl.pallas_call(
        edge_kernel,
        in_specs=[pl.BlockSpec(memory_space=pltpu.SMEM)]
        + [vmem] * 5
        + [pl.BlockSpec(memory_space=pl.ANY)]
        + [vmem] * 9,
        out_specs=[vmem, vmem],
        out_shape=[
            jax.ShapeDtypeStruct((PARTS, 128), BF16),
            jax.ShapeDtypeStruct((8 * MCAP, 128), BF16),
        ],
        scratch_shapes=[
            pltpu.VMEM((PARTS + GHOST, 128), F32),
            pltpu.VMEM((PARTS, 128), BF16),
            pltpu.VMEM((PARTS, 256), F32),
            pltpu.VMEM((64, 256), BF16),
            pltpu.VMEM((256, 256), BF16),
            pltpu.VMEM((256, 256), BF16),
            pltpu.VMEM((256, 128), BF16),
            pltpu.VMEM((256, 256), BF16),
            pltpu.VMEM((PAIR, 256), BF16),
            pltpu.VMEM((2, CHUNK, 128), BF16),
            pltpu.VMEM((4, TILE, CHUNK), BF16),
            pltpu.VMEM((4, PAIR, 256), BF16),
            pltpu.VMEM((PAIR, 256), BF16),
            pltpu.VMEM((PAIR, 256), BF16),
            pltpu.VMEM((8, 128), F32),
            pltpu.VMEM((PARTS, 128), BF16),
            pltpu.VMEM((8 * MCAP, 128), F32),
        ]
        + [pltpu.SMEM((1, CHUNK), jnp.int32)] * 4
        + [pltpu.SemaphoreType.DMA((4,))],
        compiler_params=pltpu.CompilerParams(vmem_limit_bytes=40 << 20),
        cost_estimate=pl.CostEstimate(
            flops=9_000_000_000, bytes_accessed=6_000_000, transcendentals=1_000_000
        ),
    )(brick, geom, recv, own, ghosts, dest, send, *params)


MESH = pl.DeviceIdType.MESH


def partners(count):
    floor, slab = lax.axis_index("floor"), lax.axis_index("slab")
    row, col = floor // BCOLS, floor % BCOLS
    rows = lax.axis_size("floor") // BCOLS
    slabs = lax.axis_size("slab")

    def inside(r, c):
        return (r >= 0) & (r < rows) & (c >= 0) & (c < BCOLS)

    found = []
    for dr, dc in zip(STEP_ROW, STEP_COL):
        found.append(
            (
                inside(row + dr, col + dc),
                (floor + dr * BCOLS + dc, slab),
                inside(row - dr, col - dc),
            )
        )
    found.append((slab >= 1, (floor, slab - 1), slab + 1 < slabs))
    found.append((slab + 1 < slabs, (floor, slab + 1), slab >= 1))
    return found[:count]


def greet(links):
    barrier = pltpu.get_barrier_semaphore()
    for there, device, _ in links:

        @pl.when(there)
        def _():
            pl.semaphore_signal(barrier, inc=1, device_id=device, device_id_type=MESH)


def answered(links):
    barrier = pltpu.get_barrier_semaphore()
    peers = 0
    for there, _, _ in links:
        peers = peers + there.astype(jnp.int32)
    pl.semaphore_wait(barrier, peers)


def ghost_kernel(rows_ref, own_ref, ghost_ref, table, packets, send_sems, recv_sems):
    links = partners(10)
    row8 = iota((8, 128), 0)
    ghost_ref[...] = jnp.zeros_like(ghost_ref)
    greet(links)

    @pl.loop(0, PARTS // 256)
    def _(i):
        at = pl.multiple_of(i * 256, 256)
        table[pl.ds(at, 256), :] = own_ref[pl.ds(at, 256), :].astype(F32)

    def copy(k, device):
        block = pl.ds(k * 512, 512)
        return pltpu.make_async_remote_copy(
            src_ref=packets.at[block],
            dst_ref=ghost_ref.at[block],
            send_sem=send_sems.at[k],
            recv_sem=recv_sems.at[k],
            device_id=device,
            device_id_type=MESH,
        )

    for k in (0, 2, 5, 7, 1, 6, 3, 4, 8, 9):
        there, device, _ = links[k]

        @pl.loop(0, 4)
        def _(c):
            at = pl.multiple_of(c * 128, 128)
            blocks = []
            for first in range(0, 128, 8):
                block = None
                for s in range(8):
                    line = jnp.broadcast_to(
                        table[pl.ds(rows_ref[0, k, at + first + s], 1), :], (8, 128)
                    )
                    block = line if s == 0 else jnp.where(row8 == s, line, block)
                blocks.append(block)
            packets[pl.ds(k * 512 + at, 128), :] = jnp.concatenate(blocks, axis=0).astype(BF16)

        if k == 0:
            answered(links)

        @pl.when(there)
        def _():
            copy(k, device).start()

    for k in range(10):
        there, device, comes = links[k]

        @pl.when(there)
        def _():
            copy(k, device).wait_send()

        @pl.when(comes)
        def _():
            copy(k, device).wait_recv()


def ghost_call(ghost_rows, own):
    return pl.pallas_call(
        ghost_kernel,
        in_specs=[
            pl.BlockSpec(memory_space=pltpu.SMEM),
            pl.BlockSpec(memory_space=pltpu.VMEM),
        ],
        out_specs=pl.BlockSpec(memory_space=pltpu.VMEM),
        out_shape=jax.ShapeDtypeStruct((GHOST, 128), BF16),
        scratch_shapes=[
            pltpu.VMEM((PARTS, 128), F32),
            pltpu.VMEM((GHOST, 128), BF16),
            pltpu.SemaphoreType.DMA((10,)),
            pltpu.SemaphoreType.DMA((10,)),
        ],
        compiler_params=pltpu.CompilerParams(
            collective_id=0, has_side_effects=True, vmem_limit_bytes=16 << 20
        ),
    )(ghost_rows, own)


def migrant_kernel(out_ref, arrived_ref, send_sems, recv_sems):
    links = partners(8)
    arrived_ref[...] = jnp.zeros_like(arrived_ref)

    def copy(k, device):
        return pltpu.make_async_remote_copy(
            src_ref=out_ref.at[k],
            dst_ref=arrived_ref.at[k],
            send_sem=send_sems.at[k],
            recv_sem=recv_sems.at[k],
            device_id=device,
            device_id_type=MESH,
        )

    greet(links)
    answered(links)
    for k in (0, 2, 5, 7, 1, 6, 3, 4):
        there, device, _ = links[k]

        @pl.when(there)
        def _():
            copy(k, device).start()

    for k in range(8):
        there, device, comes = links[k]

        @pl.when(there)
        def _():
            copy(k, device).wait_send()

        @pl.when(comes)
        def _():
            copy(k, device).wait_recv()


def migrant_call(outgoing):
    return pl.pallas_call(
        migrant_kernel,
        in_specs=[pl.BlockSpec(memory_space=pltpu.VMEM)],
        out_specs=pl.BlockSpec(memory_space=pltpu.VMEM),
        out_shape=jax.ShapeDtypeStruct((8, MCAP, 128), BF16),
        scratch_shapes=[pltpu.SemaphoreType.DMA((8,)), pltpu.SemaphoreType.DMA((8,))],
        compiler_params=pltpu.CompilerParams(collective_id=1, has_side_effects=True),
    )(outgoing)


def per_device(
    latent,
    edge_geom,
    edge_recv,
    edge_send,
    ghost_rows,
    dest,
    enc_w1,
    enc_b1,
    enc_w2,
    pe_w1,
    pe_w2,
    edge_gain,
    pn_w1,
    pn_w2,
    node_gain,
):
    own = latent[0]
    brick = lax.axis_index("floor").astype(jnp.int32)
    ghosts = ghost_call(ghost_rows, own)
    params = (
        enc_w1,
        enc_b1.reshape(1, 128),
        enc_w2,
        pe_w1,
        pe_w2,
        edge_gain.reshape(1, 128),
        pn_w1,
        pn_w2,
        node_gain.reshape(1, 128),
    )
    staying, outgoing = edge_call(
        brick.reshape(1), edge_geom, edge_recv, own, ghosts, dest, edge_send, params
    )
    arrived = migrant_call(outgoing.reshape(8, MCAP, 128))
    present = jnp.stack([comes for _, _, comes in partners(8)])
    arrived = jnp.where(present[:, None, None], arrived, jnp.zeros_like(arrived))
    return (staying[None], arrived[None])


def solution(mesh):
    in_specs = (
        P("slab", "floor", None),
        P("slab", None, "floor"),
        P("slab", "floor"),
        P("slab", "floor"),
        P("slab", "floor", None),
        P("slab", "floor"),
    ) + (P(),) * 9
    out_specs = (P("slab", "floor", None), P("slab", "floor", None, None))
    return jax.shard_map(
        per_device, mesh=mesh, in_specs=in_specs, out_specs=out_specs, check_vma=False
    )
```

```python
import jax
import jax.numpy as jnp
from jax import lax
from jax.experimental import pallas as pl
from jax.experimental.pallas import tpu as pltpu
from jax.sharding import PartitionSpec as P

BCOLS = 4
MCAP = 128
TILE = 128
TILES = 32
CHUNK = 1024
PAIR = 512
PER = 2048 // CHUNK
BLOCK = 1024
PARTS = 4096
GHOST = 5120
STEP_ROW = (-1, -1, -1, 0, 0, 1, 1, 1)
STEP_COL = (-1, 0, 1, -1, 1, -1, 0, 1)
EPS = 1e-05
F32 = jnp.float32
BF16 = jnp.bfloat16


def dot(a, b):
    return jnp.dot(a, b, preferred_element_type=F32)


def iota(shape, dim):
    return lax.broadcasted_iota(jnp.int32, shape, dim)


def edge_kernel(
    brick_ref,
    geom_ref,
    recv_ref,
    own_ref,
    ghost_ref,
    dest_ref,
    send_hbm,
    enc_w1_ref,
    enc_b1_ref,
    enc_w2_ref,
    pe_w1_ref,
    pe_w2_ref,
    edge_gain_ref,
    pn_w1_ref,
    pn_w2_ref,
    node_gain_ref,
    staying_ref,
    outgoing_ref,
    table,
    recv_proj,
    summed,
    w_first,
    w_enc,
    w_msg,
    w_node,
    w_mean,
    hidden,
    picked,
    picked_t,
    encoded,
    mixed,
    message,
    counts,
    updated,
    leaving,
    send_0,
    send_1,
    send_2,
    send_3,
    sems,
):
    slots = (send_0, send_1, send_2, send_3)
    chunks = TILES * PER

    def fetch(slot, chunk):
        at = jnp.clip(chunk, 0, chunks - 1) * CHUNK
        return pltpu.make_async_copy(
            send_hbm.at[:, pl.ds(pl.multiple_of(at, CHUNK), CHUNK)], slots[slot], sems.at[slot]
        )

    fetch(0, 0).start()

    w_first[...] = jnp.zeros_like(w_first)
    w_enc[...] = jnp.zeros_like(w_enc)
    w_mean[...] = jnp.zeros_like(w_mean)
    w_msg[...] = jnp.zeros_like(w_msg)
    counts[...] = jnp.zeros_like(counts)
    leaving[...] = jnp.zeros_like(leaving)
    row8 = iota((8, 128), 0)
    weights = jnp.zeros((8, 128), F32)
    for c in range(4):
        weights = jnp.where(row8 == c, enc_w1_ref[c : c + 1, :], weights)
    weights = jnp.where(row8 == 4, enc_b1_ref[0:1, :], weights)
    high = weights.astype(BF16).astype(F32)
    weights = jnp.concatenate(
        [high, high, weights - high, jnp.zeros((8, 128), F32)], axis=0
    ).astype(BF16)
    w_first[0:32, 0:128] = weights
    w_first[32:64, 128:256] = weights

    def centred(ref):
        full = ref[...].astype(F32)
        return full - jnp.mean(full, axis=1, keepdims=True)

    enc = centred(enc_w2_ref).astype(BF16)
    msg = centred(pe_w2_ref).astype(BF16)
    for k in (0, 128):
        w_enc[k : k + 128, k : k + 128] = enc
        w_mean[k : k + 128, k : k + 128] = jnp.full((128, 128), 1.0 / 128, BF16)
        w_msg[k : k + 128, k : k + 128] = msg
    full = centred(pn_w2_ref)
    high = full.astype(BF16)
    w_node[0:128, :] = high
    w_node[128:256, :] = (full - high.astype(F32)).astype(BF16)

    w_both = jnp.concatenate([pe_w1_ref[2], pe_w1_ref[1]], axis=1)

    @pl.loop(0, PARTS // 1024, unroll=2)
    def _(i):
        at = pl.multiple_of(i * 1024, 1024)
        block = dot(own_ref[pl.ds(at, 1024), :], w_both).astype(BF16)
        table[pl.ds(at, 1024), :] = block[:, 0:128].astype(F32)
        recv_proj[pl.ds(at, 1024), :] = block[:, 128:256]

    @pl.loop(0, GHOST // 1024, unroll=True)
    def _(i):
        at = pl.multiple_of(i * 1024, 1024)
        block = dot(ghost_ref[pl.ds(at, 1024), :], pe_w1_ref[2])
        table[pl.ds(PARTS + at, 1024), :] = block.astype(BF16).astype(F32)

    rows = iota((TILE, CHUNK), 0)
    r8 = iota((8, CHUNK), 0)

    def gathered(slot, first, count):
        blocks = []
        for at in range(first, first + count, 8):
            block = jnp.broadcast_to(table[pl.ds(slot[0, at], 1), :], (8, 128))
            for s in range(1, 8):
                line = jnp.broadcast_to(table[pl.ds(slot[0, at + s], 1), :], (8, 128))
                block = jnp.where(row8 == s, line, block)
            blocks.append(block)
        return jnp.concatenate(blocks, axis=0)

    def normed(values):
        spread = jnp.sum(values * values, axis=1, keepdims=True) * (1.0 / 128)
        return (values * lax.rsqrt(spread + EPS)).astype(BF16)

    def normed_pair(values):
        half = values.astype(BF16)
        spread = dot(half * half, w_mean[...])
        return (values * lax.rsqrt(spread + EPS)).astype(BF16)

    def first_layer(chunk, tile, q):
        at = pl.multiple_of(chunk * CHUNK, CHUNK)
        geom = geom_ref[0, :, pl.ds(at, CHUNK)]
        local = recv_ref[:, pl.ds(at, CHUNK)] - tile * TILE
        length = jnp.sqrt(geom[0:1] * geom[0:1] + geom[1:2] * geom[1:2] + geom[2:3] * geom[2:3])
        feats = jnp.where(r8 == 4, 1.0, jnp.zeros((8, CHUNK), F32))
        for c in range(3):
            feats = jnp.where(r8 == c, geom[c : c + 1], feats)
        feats = jnp.where(r8 == 3, length, feats)
        high = feats.astype(BF16).astype(F32)
        low = feats - high
        feats = jnp.concatenate([high, low, high, jnp.zeros_like(high)], axis=0)
        feats = jnp.concatenate([feats[:, 0:PAIR], feats[:, PAIR:CHUNK]], axis=0).astype(BF16)
        out = lax.dot_general(
            feats, w_first[...], (((0,), (0,)), ((), ())), preferred_element_type=F32
        )
        hidden[...] = jnp.maximum(out, 0.0).astype(BF16)
        picks_t = jnp.where(rows == local, 1.0, 0.0).astype(BF16)
        picked_t[q] = picks_t
        picked[q % 2] = picks_t.T

    def encode(q):
        out = dot(hidden[...], w_enc[...])
        encoded[q] = normed_pair(out)

    def mix(tile, q):
        at = pl.multiple_of(tile * TILE, TILE)
        w_mix = jnp.concatenate([pe_w1_ref[0], recv_proj[pl.ds(at, TILE), :]], axis=0)
        for side in range(2):
            lanes = slice(side * 128, side * 128 + 128)
            lhs = jnp.concatenate(
                [encoded[q, :, lanes], picked[q % 2, side * PAIR : side * PAIR + PAIR, :]], axis=1
            )
            out = dot(lhs, w_mix) + gathered(slots[q], side * PAIR, PAIR)
            mixed[:, lanes] = jnp.maximum(out, 0.0).astype(BF16)

    def messages():
        out = dot(mixed[...], w_msg[...])
        message[:, 0:128] = normed(out[:, 0:128])
        message[:, 128:256] = normed(out[:, 128:256])

    def gather_up(tile, q, first):
        out = None
        for side in range(2):
            lanes = slice(side * 128, side * 128 + 128)
            rhs = jnp.concatenate([encoded[q, :, lanes], message[:, lanes]], axis=1)
            part = dot(picked_t[q, :, side * PAIR : side * PAIR + PAIR], rhs)
            out = part if side == 0 else out + part
        at = pl.multiple_of(tile * TILE, TILE)
        if first:
            summed[pl.ds(at, TILE), :] = out
        else:
            summed[pl.ds(at, TILE), :] += out

    def body(t, q, final=False, initial=False):
        chunk = t * 4 + q

        def tile(back):
            at = t * (4 // PER) + (q - back) // PER
            return at

        live = lambda back: (not final or q < back) and (not initial or q >= back)
        if live(2):
            fetch((q - 2) % 4, chunk - 2).wait()
        if not final:
            fetch((q + 1) % 4, chunk + 1).start()
        if not initial:
            gather_up(tile(4), q, q % PER == 0)
        if live(3):
            messages()
        if live(2):
            mix(tile(2), (q - 2) % 4)
        if live(1):
            encode((q - 1) % 4)
        if live(0):
            first_layer(chunk, tile(0), q)

    for q in range(4):
        body(0, q, initial=True)

    @pl.loop(1, chunks // 4)
    def _(t):
        for q in range(4):
            body(t, q)

    for q in range(4):
        body(chunks // 4, q, final=True)
    fetch(0, chunks).wait()

    brick = brick_ref[0]
    k8 = iota((8, TILE), 0)
    k9 = jnp.where(k8 >= 4, k8 + 1, k8)
    diagonal = iota((TILE, TILE), 0) == iota((TILE, TILE), 1)
    upper = jnp.where(iota((TILE, TILE), 0) <= iota((TILE, TILE), 1), 1.0, 0.0).astype(BF16)

    w_both = jnp.concatenate([pn_w1_ref[0], pn_w1_ref[1]], axis=0)

    def node(b):
        at = pl.multiple_of(b * BLOCK, BLOCK)
        own = own_ref[pl.ds(at, BLOCK), :]
        total = summed[pl.ds(at, BLOCK), :]
        aggregate = (total[:, 0:128] + edge_gain_ref[0:1, :] * total[:, 128:256]).astype(BF16)
        out = dot(jnp.concatenate([own, aggregate], axis=1), w_both)
        out = jnp.maximum(out, 0.0).astype(BF16)
        out = dot(jnp.concatenate([out, out], axis=1), w_node[...])
        spread = jnp.sum(out * out, axis=1, keepdims=True) * (1.0 / 128)
        out = out * lax.rsqrt(spread + EPS)
        fresh = (own.astype(F32) + node_gain_ref[0:1, :] * out).astype(BF16)
        updated[pl.ds(at, BLOCK), :] = fresh
        for i in range(0, BLOCK, TILE):
            dest = dest_ref[:, pl.ds(at + i, TILE)]
            stays = jnp.where(diagonal & (dest == brick), 1.0, 0.0).astype(BF16)
            staying_ref[pl.ds(at + i, TILE), :] = dot(stays, fresh[i : i + TILE]).astype(BF16)

    def pack(b):
        at = pl.multiple_of(b * BLOCK, BLOCK)
        places = []
        seen = counts[...]
        for i in range(0, BLOCK, TILE):
            dest = dest_ref[:, pl.ds(at + i, TILE)]
            move_row = dest // BCOLS - brick // BCOLS
            move_col = dest % BCOLS - brick % BCOLS
            code = (move_row + 1) * 3 + move_col + 1
            heads = jnp.where(code == k9, 1.0, 0.0)
            running = dot(heads.astype(BF16), upper) + seen
            seen = seen + jnp.sum(heads, axis=1, keepdims=True)
            places.append(
                jnp.sum(
                    heads * (running + (k8 * MCAP).astype(F32)), axis=0, keepdims=True
                ).astype(jnp.int32) - 1
            )
        counts[...] = seen
        place = jnp.concatenate(places, axis=1)
        for k in range(0, 8 * MCAP, 256):
            chosen = jnp.where(iota((256, BLOCK), 0) + k == place, 1.0, 0.0).astype(BF16)
            leaving[k : k + 256, :] += dot(chosen, updated[pl.ds(at, BLOCK), :])

    node(0)

    @pl.loop(1, PARTS // BLOCK)
    def _(b):
        pack(b - 1)
        node(b)

    pack(PARTS // BLOCK - 1)
    outgoing_ref[...] = leaving[...].astype(BF16)


def edge_call(brick, geom, recv, own, ghosts, dest, send, params):
    vmem = pl.BlockSpec(memory_space=pltpu.VMEM)
    return pl.pallas_call(
        edge_kernel,
        in_specs=[pl.BlockSpec(memory_space=pltpu.SMEM)]
        + [vmem] * 5
        + [pl.BlockSpec(memory_space=pl.ANY)]
        + [vmem] * 9,
        out_specs=[vmem, vmem],
        out_shape=[
            jax.ShapeDtypeStruct((PARTS, 128), BF16),
            jax.ShapeDtypeStruct((8 * MCAP, 128), BF16),
        ],
        scratch_shapes=[
            pltpu.VMEM((PARTS + GHOST, 128), F32),
            pltpu.VMEM((PARTS, 128), BF16),
            pltpu.VMEM((PARTS, 256), F32),
            pltpu.VMEM((64, 256), BF16),
            pltpu.VMEM((256, 256), BF16),
            pltpu.VMEM((256, 256), BF16),
            pltpu.VMEM((256, 128), BF16),
            pltpu.VMEM((256, 256), BF16),
            pltpu.VMEM((PAIR, 256), BF16),
            pltpu.VMEM((2, CHUNK, 128), BF16),
            pltpu.VMEM((4, TILE, CHUNK), BF16),
            pltpu.VMEM((4, PAIR, 256), BF16),
            pltpu.VMEM((PAIR, 256), BF16),
            pltpu.VMEM((PAIR, 256), BF16),
            pltpu.VMEM((8, 128), F32),
            pltpu.VMEM((PARTS, 128), BF16),
            pltpu.VMEM((8 * MCAP, 128), F32),
        ]
        + [pltpu.SMEM((1, CHUNK), jnp.int32)] * 4
        + [pltpu.SemaphoreType.DMA((4,))],
        compiler_params=pltpu.CompilerParams(vmem_limit_bytes=40 << 20),
        cost_estimate=pl.CostEstimate(
            flops=9_000_000_000, bytes_accessed=6_000_000, transcendentals=1_000_000
        ),
    )(brick, geom, recv, own, ghosts, dest, send, *params)


MESH = pl.DeviceIdType.MESH


def partners(count):
    floor, slab = lax.axis_index("floor"), lax.axis_index("slab")
    row, col = floor // BCOLS, floor % BCOLS
    rows = lax.axis_size("floor") // BCOLS
    slabs = lax.axis_size("slab")

    def inside(r, c):
        return (r >= 0) & (r < rows) & (c >= 0) & (c < BCOLS)

    found = []
    for dr, dc in zip(STEP_ROW, STEP_COL):
        found.append(
            (
                inside(row + dr, col + dc),
                (floor + dr * BCOLS + dc, slab),
                inside(row - dr, col - dc),
            )
        )
    found.append((slab >= 1, (floor, slab - 1), slab + 1 < slabs))
    found.append((slab + 1 < slabs, (floor, slab + 1), slab >= 1))
    return found[:count]


def greet(links):
    barrier = pltpu.get_barrier_semaphore()
    for there, device, _ in links:

        @pl.when(there)
        def _():
            pl.semaphore_signal(barrier, inc=1, device_id=device, device_id_type=MESH)


def answered(links):
    barrier = pltpu.get_barrier_semaphore()
    peers = 0
    for there, _, _ in links:
        peers = peers + there.astype(jnp.int32)
    pl.semaphore_wait(barrier, peers)


def ghost_kernel(rows_ref, own_ref, ghost_ref, table, packets, send_sems, recv_sems):
    links = partners(10)
    row8 = iota((8, 128), 0)
    ghost_ref[...] = jnp.zeros_like(ghost_ref)
    greet(links)

    @pl.loop(0, PARTS // 256)
    def _(i):
        at = pl.multiple_of(i * 256, 256)
        table[pl.ds(at, 256), :] = own_ref[pl.ds(at, 256), :].astype(F32)

    def copy(k, device):
        block = pl.ds(k * 512, 512)
        return pltpu.make_async_remote_copy(
            src_ref=packets.at[block],
            dst_ref=ghost_ref.at[block],
            send_sem=send_sems.at[k],
            recv_sem=recv_sems.at[k],
            device_id=device,
            device_id_type=MESH,
        )

    for k in (0, 2, 5, 7, 1, 6, 3, 4, 8, 9):
        there, device, _ = links[k]

        @pl.loop(0, 4)
        def _(c):
            at = pl.multiple_of(c * 128, 128)
            blocks = []
            for first in range(0, 128, 8):
                block = None
                for s in range(8):
                    line = jnp.broadcast_to(
                        table[pl.ds(rows_ref[0, k, at + first + s], 1), :], (8, 128)
                    )
                    block = line if s == 0 else jnp.where(row8 == s, line, block)
                blocks.append(block)
            packets[pl.ds(k * 512 + at, 128), :] = jnp.concatenate(blocks, axis=0).astype(BF16)

        if k == 0:
            answered(links)

        @pl.when(there)
        def _():
            copy(k, device).start()

    for k in range(10):
        there, device, comes = links[k]

        @pl.when(there)
        def _():
            copy(k, device).wait_send()

        @pl.when(comes)
        def _():
            copy(k, device).wait_recv()


def ghost_call(ghost_rows, own):
    return pl.pallas_call(
        ghost_kernel,
        in_specs=[
            pl.BlockSpec(memory_space=pltpu.SMEM),
            pl.BlockSpec(memory_space=pltpu.VMEM),
        ],
        out_specs=pl.BlockSpec(memory_space=pltpu.VMEM),
        out_shape=jax.ShapeDtypeStruct((GHOST, 128), BF16),
        scratch_shapes=[
            pltpu.VMEM((PARTS, 128), F32),
            pltpu.VMEM((GHOST, 128), BF16),
            pltpu.SemaphoreType.DMA((10,)),
            pltpu.SemaphoreType.DMA((10,)),
        ],
        compiler_params=pltpu.CompilerParams(
            collective_id=0, has_side_effects=True, vmem_limit_bytes=16 << 20
        ),
    )(ghost_rows, own)


def migrant_kernel(out_ref, arrived_ref, send_sems, recv_sems):
    links = partners(8)
    arrived_ref[...] = jnp.zeros_like(arrived_ref)

    def copy(k, device):
        return pltpu.make_async_remote_copy(
            src_ref=out_ref.at[k],
            dst_ref=arrived_ref.at[k],
            send_sem=send_sems.at[k],
            recv_sem=recv_sems.at[k],
            device_id=device,
            device_id_type=MESH,
        )

    greet(links)
    answered(links)
    for k in (0, 2, 5, 7, 1, 6, 3, 4):
        there, device, _ = links[k]

        @pl.when(there)
        def _():
            copy(k, device).start()

    for k in range(8):
        there, device, comes = links[k]

        @pl.when(there)
        def _():
            copy(k, device).wait_send()

        @pl.when(comes)
        def _():
            copy(k, device).wait_recv()


def migrant_call(outgoing):
    return pl.pallas_call(
        migrant_kernel,
        in_specs=[pl.BlockSpec(memory_space=pltpu.VMEM)],
        out_specs=pl.BlockSpec(memory_space=pltpu.VMEM),
        out_shape=jax.ShapeDtypeStruct((8, MCAP, 128), BF16),
        scratch_shapes=[pltpu.SemaphoreType.DMA((8,)), pltpu.SemaphoreType.DMA((8,))],
        compiler_params=pltpu.CompilerParams(collective_id=1, has_side_effects=True),
    )(outgoing)


def per_device(
    latent,
    edge_geom,
    edge_recv,
    edge_send,
    ghost_rows,
    dest,
    enc_w1,
    enc_b1,
    enc_w2,
    pe_w1,
    pe_w2,
    edge_gain,
    pn_w1,
    pn_w2,
    node_gain,
):
    own = latent[0]
    brick = lax.axis_index("floor").astype(jnp.int32)
    ghosts = ghost_call(ghost_rows, own)
    params = (
        enc_w1,
        enc_b1.reshape(1, 128),
        enc_w2,
        pe_w1,
        pe_w2,
        edge_gain.reshape(1, 128),
        pn_w1,
        pn_w2,
        node_gain.reshape(1, 128),
    )
    staying, outgoing = edge_call(
        brick.reshape(1), edge_geom, edge_recv, own, ghosts, dest, edge_send, params
    )
    arrived = migrant_call(outgoing.reshape(8, MCAP, 128))
    present = jnp.stack([comes for _, _, comes in partners(8)])
    arrived = jnp.where(present[:, None, None], arrived, jnp.zeros_like(arrived))
    return (staying[None], arrived[None])


def solution(mesh):
    in_specs = (
        P("slab", "floor", None),
        P("slab", None, "floor"),
        P("slab", "floor"),
        P("slab", "floor"),
        P("slab", "floor", None),
        P("slab", "floor"),
    ) + (P(),) * 9
    out_specs = (P("slab", "floor", None), P("slab", "floor", None, None))
    return jax.shard_map(
        per_device, mesh=mesh, in_specs=in_specs, out_specs=out_specs, check_vma=False
    )
```

```python
import jax
import jax.numpy as jnp
from jax import lax
from jax.experimental import pallas as pl
from jax.experimental.pallas import tpu as pltpu
from jax.sharding import PartitionSpec as P

BCOLS = 4
MCAP = 128
TILE = 128
TILES = 32
CHUNK = 1024
PAIR = 512
PER = 2048 // CHUNK
BLOCK = 2048
PARTS = 4096
GHOST = 5120
STEP_ROW = (-1, -1, -1, 0, 0, 1, 1, 1)
STEP_COL = (-1, 0, 1, -1, 1, -1, 0, 1)
EPS = 1e-05
F32 = jnp.float32
BF16 = jnp.bfloat16


def dot(a, b):
    return jnp.dot(a, b, preferred_element_type=F32)


def iota(shape, dim):
    return lax.broadcasted_iota(jnp.int32, shape, dim)


def edge_kernel(
    brick_ref,
    geom_ref,
    recv_ref,
    own_ref,
    ghost_ref,
    dest_ref,
    send_hbm,
    enc_w1_ref,
    enc_b1_ref,
    enc_w2_ref,
    pe_w1_ref,
    pe_w2_ref,
    edge_gain_ref,
    pn_w1_ref,
    pn_w2_ref,
    node_gain_ref,
    staying_ref,
    outgoing_ref,
    table,
    recv_proj,
    summed,
    w_first,
    w_enc,
    w_msg,
    w_node,
    w_mean,
    hidden,
    picked,
    picked_t,
    encoded,
    mixed,
    message,
    counts,
    updated,
    leaving,
    send_0,
    send_1,
    send_2,
    send_3,
    sems,
):
    slots = (send_0, send_1, send_2, send_3)
    chunks = TILES * PER

    def fetch(slot, chunk):
        at = jnp.clip(chunk, 0, chunks - 1) * CHUNK
        return pltpu.make_async_copy(
            send_hbm.at[:, pl.ds(pl.multiple_of(at, CHUNK), CHUNK)], slots[slot], sems.at[slot]
        )

    fetch(0, 0).start()

    w_first[...] = jnp.zeros_like(w_first)
    w_enc[...] = jnp.zeros_like(w_enc)
    w_mean[...] = jnp.zeros_like(w_mean)
    w_msg[...] = jnp.zeros_like(w_msg)
    counts[...] = jnp.zeros_like(counts)
    leaving[...] = jnp.zeros_like(leaving)
    row8 = iota((8, 128), 0)
    weights = jnp.zeros((8, 128), F32)
    for c in range(4):
        weights = jnp.where(row8 == c, enc_w1_ref[c : c + 1, :], weights)
    weights = jnp.where(row8 == 4, enc_b1_ref[0:1, :], weights)
    high = weights.astype(BF16).astype(F32)
    weights = jnp.concatenate(
        [high, high, weights - high, jnp.zeros((8, 128), F32)], axis=0
    ).astype(BF16)
    w_first[0:32, 0:128] = weights
    w_first[32:64, 128:256] = weights

    def centred(ref):
        full = ref[...].astype(F32)
        return full - jnp.mean(full, axis=1, keepdims=True)

    enc = centred(enc_w2_ref).astype(BF16)
    msg = centred(pe_w2_ref).astype(BF16)
    for k in (0, 128):
        w_enc[k : k + 128, k : k + 128] = enc
        w_mean[k : k + 128, k : k + 128] = jnp.full((128, 128), 1.0 / 128, BF16)
        w_msg[k : k + 128, k : k + 128] = msg
    full = centred(pn_w2_ref)
    high = full.astype(BF16)
    w_node[0:128, :] = high
    w_node[128:256, :] = (full - high.astype(F32)).astype(BF16)

    w_both = jnp.concatenate([pe_w1_ref[2], pe_w1_ref[1]], axis=1)

    @pl.loop(0, PARTS // 1024, unroll=2)
    def _(i):
        at = pl.multiple_of(i * 1024, 1024)
        block = dot(own_ref[pl.ds(at, 1024), :], w_both).astype(BF16)
        table[pl.ds(at, 1024), :] = block[:, 0:128].astype(F32)
        recv_proj[pl.ds(at, 1024), :] = block[:, 128:256]

    @pl.loop(0, GHOST // 1024, unroll=True)
    def _(i):
        at = pl.multiple_of(i * 1024, 1024)
        block = dot(ghost_ref[pl.ds(at, 1024), :], pe_w1_ref[2])
        table[pl.ds(PARTS + at, 1024), :] = block.astype(BF16).astype(F32)

    rows = iota((TILE, CHUNK), 0)
    r8 = iota((8, CHUNK), 0)

    def gathered(slot, first, count):
        blocks = []
        for at in range(first, first + count, 8):
            block = jnp.broadcast_to(table[pl.ds(slot[0, at], 1), :], (8, 128))
            for s in range(1, 8):
                line = jnp.broadcast_to(table[pl.ds(slot[0, at + s], 1), :], (8, 128))
                block = jnp.where(row8 == s, line, block)
            blocks.append(block)
        return jnp.concatenate(blocks, axis=0)

    def normed(values):
        spread = jnp.sum(values * values, axis=1, keepdims=True) * (1.0 / 128)
        return (values * lax.rsqrt(spread + EPS)).astype(BF16)

    def normed_pair(values):
        half = values.astype(BF16)
        spread = dot(half * half, w_mean[...])
        return (values * lax.rsqrt(spread + EPS)).astype(BF16)

    def first_layer(chunk, tile, q):
        at = pl.multiple_of(chunk * CHUNK, CHUNK)
        geom = geom_ref[0, :, pl.ds(at, CHUNK)]
        local = recv_ref[:, pl.ds(at, CHUNK)] - tile * TILE
        length = jnp.sqrt(geom[0:1] * geom[0:1] + geom[1:2] * geom[1:2] + geom[2:3] * geom[2:3])
        feats = jnp.where(r8 == 4, 1.0, jnp.zeros((8, CHUNK), F32))
        for c in range(3):
            feats = jnp.where(r8 == c, geom[c : c + 1], feats)
        feats = jnp.where(r8 == 3, length, feats)
        high = feats.astype(BF16).astype(F32)
        low = feats - high
        feats = jnp.concatenate([high, low, high, jnp.zeros_like(high)], axis=0)
        feats = jnp.concatenate([feats[:, 0:PAIR], feats[:, PAIR:CHUNK]], axis=0).astype(BF16)
        out = lax.dot_general(
            feats, w_first[...], (((0,), (0,)), ((), ())), preferred_element_type=F32
        )
        hidden[...] = jnp.maximum(out, 0.0).astype(BF16)
        picks_t = jnp.where(rows == local, 1.0, 0.0).astype(BF16)
        picked_t[q] = picks_t
        picked[q % 2] = picks_t.T

    def encode(q):
        out = dot(hidden[...], w_enc[...])
        encoded[q] = normed_pair(out)

    def mix(tile, q):
        at = pl.multiple_of(tile * TILE, TILE)
        w_mix = jnp.concatenate([pe_w1_ref[0], recv_proj[pl.ds(at, TILE), :]], axis=0)
        for side in range(2):
            lanes = slice(side * 128, side * 128 + 128)
            lhs = jnp.concatenate(
                [encoded[q, :, lanes], picked[q % 2, side * PAIR : side * PAIR + PAIR, :]], axis=1
            )
            out = dot(lhs, w_mix) + gathered(slots[q], side * PAIR, PAIR)
            mixed[:, lanes] = jnp.maximum(out, 0.0).astype(BF16)

    def messages():
        out = dot(mixed[...], w_msg[...])
        message[:, 0:128] = normed(out[:, 0:128])
        message[:, 128:256] = normed(out[:, 128:256])

    def gather_up(tile, q, first):
        out = None
        for side in range(2):
            lanes = slice(side * 128, side * 128 + 128)
            rhs = jnp.concatenate([encoded[q, :, lanes], message[:, lanes]], axis=1)
            part = dot(picked_t[q, :, side * PAIR : side * PAIR + PAIR], rhs)
            out = part if side == 0 else out + part
        at = pl.multiple_of(tile * TILE, TILE)
        if first:
            summed[pl.ds(at, TILE), :] = out
        else:
            summed[pl.ds(at, TILE), :] += out

    def body(t, q, final=False, initial=False):
        chunk = t * 4 + q

        def tile(back):
            at = t * (4 // PER) + (q - back) // PER
            return at

        live = lambda back: (not final or q < back) and (not initial or q >= back)
        if live(2):
            fetch((q - 2) % 4, chunk - 2).wait()
        if not final:
            fetch((q + 1) % 4, chunk + 1).start()
        if not initial:
            gather_up(tile(4), q, q % PER == 0)
        if live(3):
            messages()
        if live(2):
            mix(tile(2), (q - 2) % 4)
        if live(1):
            encode((q - 1) % 4)
        if live(0):
            first_layer(chunk, tile(0), q)

    for q in range(4):
        body(0, q, initial=True)

    @pl.loop(1, chunks // 4)
    def _(t):
        for q in range(4):
            body(t, q)

    for q in range(4):
        body(chunks // 4, q, final=True)
    fetch(0, chunks).wait()

    brick = brick_ref[0]
    k8 = iota((8, TILE), 0)
    k9 = jnp.where(k8 >= 4, k8 + 1, k8)
    diagonal = iota((TILE, TILE), 0) == iota((TILE, TILE), 1)
    upper = jnp.where(iota((TILE, TILE), 0) <= iota((TILE, TILE), 1), 1.0, 0.0).astype(BF16)

    w_both = jnp.concatenate([pn_w1_ref[0], pn_w1_ref[1]], axis=0)

    def node(b):
        at = pl.multiple_of(b * BLOCK, BLOCK)
        own = own_ref[pl.ds(at, BLOCK), :]
        total = summed[pl.ds(at, BLOCK), :]
        aggregate = (total[:, 0:128] + edge_gain_ref[0:1, :] * total[:, 128:256]).astype(BF16)
        out = dot(jnp.concatenate([own, aggregate], axis=1), w_both)
        out = jnp.maximum(out, 0.0).astype(BF16)
        out = dot(jnp.concatenate([out, out], axis=1), w_node[...])
        spread = jnp.sum(out * out, axis=1, keepdims=True) * (1.0 / 128)
        out = out * lax.rsqrt(spread + EPS)
        fresh = (own.astype(F32) + node_gain_ref[0:1, :] * out).astype(BF16)
        updated[pl.ds(at, BLOCK), :] = fresh
        for i in range(0, BLOCK, TILE):
            dest = dest_ref[:, pl.ds(at + i, TILE)]
            stays = jnp.where(diagonal & (dest == brick), 1.0, 0.0).astype(BF16)
            staying_ref[pl.ds(at + i, TILE), :] = dot(stays, fresh[i : i + TILE]).astype(BF16)

    def pack(b):
        at = pl.multiple_of(b * BLOCK, BLOCK)
        places = []
        seen = counts[...]
        for i in range(0, BLOCK, TILE):
            dest = dest_ref[:, pl.ds(at + i, TILE)]
            move_row = dest // BCOLS - brick // BCOLS
            move_col = dest % BCOLS - brick % BCOLS
            code = (move_row + 1) * 3 + move_col + 1
            heads = jnp.where(code == k9, 1.0, 0.0)
            running = dot(heads.astype(BF16), upper) + seen
            seen = seen + jnp.sum(heads, axis=1, keepdims=True)
            places.append(
                jnp.sum(
                    heads * (running + (k8 * MCAP).astype(F32)), axis=0, keepdims=True
                ).astype(jnp.int32) - 1
            )
        counts[...] = seen
        place = jnp.concatenate(places, axis=1)
        for k in range(0, 8 * MCAP, 256):
            chosen = jnp.where(iota((256, BLOCK), 0) + k == place, 1.0, 0.0).astype(BF16)
            leaving[k : k + 256, :] += dot(chosen, updated[pl.ds(at, BLOCK), :])

    node(0)

    @pl.loop(1, PARTS // BLOCK)
    def _(b):
        pack(b - 1)
        node(b)

    pack(PARTS // BLOCK - 1)
    outgoing_ref[...] = leaving[...].astype(BF16)


def edge_call(brick, geom, recv, own, ghosts, dest, send, params):
    vmem = pl.BlockSpec(memory_space=pltpu.VMEM)
    return pl.pallas_call(
        edge_kernel,
        in_specs=[pl.BlockSpec(memory_space=pltpu.SMEM)]
        + [vmem] * 5
        + [pl.BlockSpec(memory_space=pl.ANY)]
        + [vmem] * 9,
        out_specs=[vmem, vmem],
        out_shape=[
            jax.ShapeDtypeStruct((PARTS, 128), BF16),
            jax.ShapeDtypeStruct((8 * MCAP, 128), BF16),
        ],
        scratch_shapes=[
            pltpu.VMEM((PARTS + GHOST, 128), F32),
            pltpu.VMEM((PARTS, 128), BF16),
            pltpu.VMEM((PARTS, 256), F32),
            pltpu.VMEM((64, 256), BF16),
            pltpu.VMEM((256, 256), BF16),
            pltpu.VMEM((256, 256), BF16),
            pltpu.VMEM((256, 128), BF16),
            pltpu.VMEM((256, 256), BF16),
            pltpu.VMEM((PAIR, 256), BF16),
            pltpu.VMEM((2, CHUNK, 128), BF16),
            pltpu.VMEM((4, TILE, CHUNK), BF16),
            pltpu.VMEM((4, PAIR, 256), BF16),
            pltpu.VMEM((PAIR, 256), BF16),
            pltpu.VMEM((PAIR, 256), BF16),
            pltpu.VMEM((8, 128), F32),
            pltpu.VMEM((PARTS, 128), BF16),
            pltpu.VMEM((8 * MCAP, 128), F32),
        ]
        + [pltpu.SMEM((1, CHUNK), jnp.int32)] * 4
        + [pltpu.SemaphoreType.DMA((4,))],
        compiler_params=pltpu.CompilerParams(vmem_limit_bytes=40 << 20),
        cost_estimate=pl.CostEstimate(
            flops=9_000_000_000, bytes_accessed=6_000_000, transcendentals=1_000_000
        ),
    )(brick, geom, recv, own, ghosts, dest, send, *params)


MESH = pl.DeviceIdType.MESH


def partners(count):
    floor, slab = lax.axis_index("floor"), lax.axis_index("slab")
    row, col = floor // BCOLS, floor % BCOLS
    rows = lax.axis_size("floor") // BCOLS
    slabs = lax.axis_size("slab")

    def inside(r, c):
        return (r >= 0) & (r < rows) & (c >= 0) & (c < BCOLS)

    found = []
    for dr, dc in zip(STEP_ROW, STEP_COL):
        found.append(
            (
                inside(row + dr, col + dc),
                (floor + dr * BCOLS + dc, slab),
                inside(row - dr, col - dc),
            )
        )
    found.append((slab >= 1, (floor, slab - 1), slab + 1 < slabs))
    found.append((slab + 1 < slabs, (floor, slab + 1), slab >= 1))
    return found[:count]


def greet(links):
    barrier = pltpu.get_barrier_semaphore()
    for there, device, _ in links:

        @pl.when(there)
        def _():
            pl.semaphore_signal(barrier, inc=1, device_id=device, device_id_type=MESH)


def answered(links):
    barrier = pltpu.get_barrier_semaphore()
    peers = 0
    for there, _, _ in links:
        peers = peers + there.astype(jnp.int32)
    pl.semaphore_wait(barrier, peers)


def ghost_kernel(rows_ref, own_ref, ghost_ref, table, packets, send_sems, recv_sems):
    links = partners(10)
    row8 = iota((8, 128), 0)
    ghost_ref[...] = jnp.zeros_like(ghost_ref)
    greet(links)

    @pl.loop(0, PARTS // 256)
    def _(i):
        at = pl.multiple_of(i * 256, 256)
        table[pl.ds(at, 256), :] = own_ref[pl.ds(at, 256), :].astype(F32)

    def copy(k, device):
        block = pl.ds(k * 512, 512)
        return pltpu.make_async_remote_copy(
            src_ref=packets.at[block],
            dst_ref=ghost_ref.at[block],
            send_sem=send_sems.at[k],
            recv_sem=recv_sems.at[k],
            device_id=device,
            device_id_type=MESH,
        )

    for k in (0, 2, 5, 7, 1, 6, 3, 4, 8, 9):
        there, device, _ = links[k]

        @pl.loop(0, 4)
        def _(c):
            at = pl.multiple_of(c * 128, 128)
            blocks = []
            for first in range(0, 128, 8):
                block = None
                for s in range(8):
                    line = jnp.broadcast_to(
                        table[pl.ds(rows_ref[0, k, at + first + s], 1), :], (8, 128)
                    )
                    block = line if s == 0 else jnp.where(row8 == s, line, block)
                blocks.append(block)
            packets[pl.ds(k * 512 + at, 128), :] = jnp.concatenate(blocks, axis=0).astype(BF16)

        if k == 0:
            answered(links)

        @pl.when(there)
        def _():
            copy(k, device).start()

    for k in range(10):
        there, device, comes = links[k]

        @pl.when(there)
        def _():
            copy(k, device).wait_send()

        @pl.when(comes)
        def _():
            copy(k, device).wait_recv()


def ghost_call(ghost_rows, own):
    return pl.pallas_call(
        ghost_kernel,
        in_specs=[
            pl.BlockSpec(memory_space=pltpu.SMEM),
            pl.BlockSpec(memory_space=pltpu.VMEM),
        ],
        out_specs=pl.BlockSpec(memory_space=pltpu.VMEM),
        out_shape=jax.ShapeDtypeStruct((GHOST, 128), BF16),
        scratch_shapes=[
            pltpu.VMEM((PARTS, 128), F32),
            pltpu.VMEM((GHOST, 128), BF16),
            pltpu.SemaphoreType.DMA((10,)),
            pltpu.SemaphoreType.DMA((10,)),
        ],
        compiler_params=pltpu.CompilerParams(
            collective_id=0, has_side_effects=True, vmem_limit_bytes=16 << 20
        ),
    )(ghost_rows, own)


def migrant_kernel(out_ref, arrived_ref, send_sems, recv_sems):
    links = partners(8)
    arrived_ref[...] = jnp.zeros_like(arrived_ref)

    def copy(k, device):
        return pltpu.make_async_remote_copy(
            src_ref=out_ref.at[k],
            dst_ref=arrived_ref.at[k],
            send_sem=send_sems.at[k],
            recv_sem=recv_sems.at[k],
            device_id=device,
            device_id_type=MESH,
        )

    greet(links)
    answered(links)
    for k in (0, 2, 5, 7, 1, 6, 3, 4):
        there, device, _ = links[k]

        @pl.when(there)
        def _():
            copy(k, device).start()

    for k in range(8):
        there, device, comes = links[k]

        @pl.when(there)
        def _():
            copy(k, device).wait_send()

        @pl.when(comes)
        def _():
            copy(k, device).wait_recv()


def migrant_call(outgoing):
    return pl.pallas_call(
        migrant_kernel,
        in_specs=[pl.BlockSpec(memory_space=pltpu.VMEM)],
        out_specs=pl.BlockSpec(memory_space=pltpu.VMEM),
        out_shape=jax.ShapeDtypeStruct((8, MCAP, 128), BF16),
        scratch_shapes=[pltpu.SemaphoreType.DMA((8,)), pltpu.SemaphoreType.DMA((8,))],
        compiler_params=pltpu.CompilerParams(collective_id=1, has_side_effects=True),
    )(outgoing)


def per_device(
    latent,
    edge_geom,
    edge_recv,
    edge_send,
    ghost_rows,
    dest,
    enc_w1,
    enc_b1,
    enc_w2,
    pe_w1,
    pe_w2,
    edge_gain,
    pn_w1,
    pn_w2,
    node_gain,
):
    own = latent[0]
    brick = lax.axis_index("floor").astype(jnp.int32)
    ghosts = ghost_call(ghost_rows, own)
    params = (
        enc_w1,
        enc_b1.reshape(1, 128),
        enc_w2,
        pe_w1,
        pe_w2,
        edge_gain.reshape(1, 128),
        pn_w1,
        pn_w2,
        node_gain.reshape(1, 128),
    )
    staying, outgoing = edge_call(
        brick.reshape(1), edge_geom, edge_recv, own, ghosts, dest, edge_send, params
    )
    arrived = migrant_call(outgoing.reshape(8, MCAP, 128))
    present = jnp.stack([comes for _, _, comes in partners(8)])
    arrived = jnp.where(present[:, None, None], arrived, jnp.zeros_like(arrived))
    return (staying[None], arrived[None])


def solution(mesh):
    in_specs = (
        P("slab", "floor", None),
        P("slab", None, "floor"),
        P("slab", "floor"),
        P("slab", "floor"),
        P("slab", "floor", None),
        P("slab", "floor"),
    ) + (P(),) * 9
    out_specs = (P("slab", "floor", None), P("slab", "floor", None, None))
    return jax.shard_map(
        per_device, mesh=mesh, in_specs=in_specs, out_specs=out_specs, check_vma=False
    )
```
